32 devices in a mesh: groups: 2 (over x), dp: 16 (over z, y, core).
Axes of the slice: x: 2, y: 2, z: 4, core: 2. Of those that a mesh axis runs over, the one named last changes fastest.
Arguments:
- hidden_input_rows: bfloat16 [8192, 8192], P(('groups', 'dp')), parts along dimension 0, may hold values from -6 to 6
- rank_cotangent: bfloat16 [8192, 128], P(('groups', 'dp')), parts along dimension 0, may hold values from -0.25 to 0.25
- token_identifiers: int32 [8192], P(('groups', 'dp')), parts along dimension 0, may hold values from 0 to 31999, as said below
- adam_first_moment: float32 [8192, 128], P('dp'), may hold values from -0.6 to 0.6
- adam_second_moment: float32 [8192, 128], P('dp'), may hold values from 0.0001 to 0.01
- block_seeds: int32 [8], replicated, may hold values from 0 to 1073741823
Outputs:
- feature_rows: float32 [32, 2048], P(('groups', 'dp')), parts along dimension 0
The draws below stay inside these ranges and needn't reach their ends.
There are 2 independent parts, one for each index of `groups`. The reference program is written for one: setup_inputs(seed, part) draws one part's arguments, and reference() takes and returns one part's arrays. A program takes and returns all parts, laid end to end along the dimension named above; an argument that names none is the same for every part. Nothing has to cross between parts.
Inputs may be any that keep to these rules, and one draw needn't show every extreme that they name: `token_identifiers`: 0 marks padding. In each sequence of 512 positions the real tokens (ids 1 and up) come first and number at least 128; the rest is padding. Some sequence has no padding.
All inputs are finite; a program needn't handle non-finite values.
Results may differ from the reference program's by a relative error of at most 0.0029.
Values sent between devices are 32-bit elements; how exact they have to be, the bound alone decides.
A program may use at most 64 MiB of HBM per device.

```python
import math
import jax
import jax.numpy as jnp
from jax import lax

D = 8192
VOCAB = 32000
ADAPTER_RANK = 128
K = 4096
FEAT_BLOCK = 512
SEQ_LEN = 512
SEQS = 8
TOKEN_TOTAL = 4096


def draw_token_identifiers(key, part):
    key_lengths = jax.random.fold_in(key, 11)
    key_full = jax.random.fold_in(key, 12)
    key_values = jax.random.fold_in(key, 13)
    lengths = jax.random.randint(key_lengths, (SEQS,), SEQ_LEN // 4, SEQ_LEN + 1, dtype=jnp.int32)
    full_row = jax.random.randint(key_full, (), 0, SEQS, dtype=jnp.int32)
    lengths = jnp.where(jnp.arange(SEQS, dtype=jnp.int32) == full_row, SEQ_LEN, lengths)
    token_values = jax.random.randint(key_values, (SEQS, SEQ_LEN), 1, VOCAB, dtype=jnp.int32)
    positions = jnp.arange(SEQ_LEN, dtype=jnp.int32)[None, :]
    return jnp.where(positions < lengths[:, None], token_values, 0).reshape(TOKEN_TOTAL)


def plant(values, key, smallest, top_value):
    shape = values.shape
    index_at = [jax.random.randint(jax.random.fold_in(key, axis), (), 0, shape[axis]) for axis in range(len(shape))]
    values = values.at[tuple(index_at)].set(smallest)
    longest = shape.index(max(shape))
    index_at[longest] = (index_at[longest] + 1) % shape[longest]
    return values.at[tuple(index_at)].set(top_value)


def block_scale(key, extent, pieces, smallest, high):
    def one(axis_at, parts):
        steps = jax.random.uniform(jax.random.fold_in(jax.random.fold_in(key, 6), axis_at), (parts,), jnp.float32, smallest / len(pieces), high / len(pieces))
        return jnp.repeat(jnp.exp(steps), extent[axis_at] // parts).reshape((-1,) + (1,) * (len(extent) - axis_at - 1))

    gain = one(*pieces[0])
    for cut in pieces[1:]:
        gain = gain * one(*cut)
    return gain


def centred(stream_key, dims, scale, limit, pieces=(), held_as=jnp.bfloat16):
    gain = block_scale(stream_key, dims, pieces, -0.22, 0.18) if pieces else 1.0
    entries = jax.random.normal(stream_key, dims, jnp.float32) * scale * gain
    return jnp.minimum(jnp.maximum(entries, -limit), limit).astype(held_as)


def setup_inputs(seed: int = 0, part: int = 0) -> dict:
    streams_of = jax.random.split(jax.random.key(seed), 7)
    part_splits = jax.random.split(jax.random.fold_in(streams_of[6], part), 7)
    hidden_input_rows = centred(part_splits[0], (TOKEN_TOTAL, D), 1.0, 6.0, ((0, 16),))
    rank_cotangent = centred(part_splits[1], (TOKEN_TOTAL, ADAPTER_RANK), 0.03125, 0.25, ((0, 16),))
    token_identifiers = draw_token_identifiers(jax.random.fold_in(jax.random.fold_in(streams_of[6], part), 71), part)
    adam_first_moment = centred(streams_of[3], (D, ADAPTER_RANK), 0.1, 0.6, ((0, 16),), jnp.float32)
    adam_second_moment = jnp.clip(jnp.exp(math.log(0.01) - 4.6051702 * jax.random.uniform(streams_of[4], (D, ADAPTER_RANK), jnp.float32) ** block_scale(streams_of[4], (D, ADAPTER_RANK), ((0, 16),), -0.2, 0.2)), 0.0001, 0.01)
    block_seeds = plant(jax.random.randint(streams_of[5], (K // FEAT_BLOCK,), 0, 1073741824), jax.random.fold_in(streams_of[5], 1), 0, 1073741823).astype(jnp.int32)
    return {"hidden_input_rows": hidden_input_rows, "rank_cotangent": rank_cotangent, "token_identifiers": token_identifiers, "adam_first_moment": adam_first_moment, "adam_second_moment": adam_second_moment, "block_seeds": block_seeds}


beta_one = 0.9
beta_two = 0.999
epsilon = 1e-08
mix_feature = 1640531527
mix_param = 2028178513
mix_round = 73244475

def scramble(hashed):
    hashed = hashed ^ lax.shift_right_logical(hashed, jnp.full_like(hashed, 16))
    hashed = hashed * mix_round
    hashed = hashed ^ lax.shift_right_logical(hashed, jnp.full_like(hashed, 16))
    hashed = hashed * mix_round
    hashed = hashed ^ lax.shift_right_logical(hashed, jnp.full_like(hashed, 16))
    return hashed

def sign_block(seed_values, feature_index, param_index):
    hashed = seed_values[:, None] + feature_index[:, None] * mix_feature + param_index[None, :] * mix_param
    hashed = scramble(hashed)
    return 1 - 2 * lax.shift_right_logical(hashed, jnp.full_like(hashed, 31))

def reference(hidden_input_rows, rank_cotangent, token_identifiers, adam_first_moment, adam_second_moment, block_seeds):
    padding_mask = (token_identifiers != 0).astype(jnp.bfloat16)
    masked_values = rank_cotangent * padding_mask[:, None]
    inputs_seq = hidden_input_rows.reshape(SEQS, SEQ_LEN, D)
    masked_seq = masked_values.reshape(SEQS, SEQ_LEN, ADAPTER_RANK)

    def one_grad(pair_args):
        return jnp.dot(pair_args[0].T, pair_args[1], preferred_element_type=jnp.float32)
    gradient = lax.map(one_grad, (inputs_seq, masked_seq))
    moment_one = beta_one * adam_first_moment[None] + (1 - beta_one) * gradient
    moment_two = beta_two * adam_second_moment[None] + (1 - beta_two) * gradient * gradient
    direction = (moment_one / (jnp.sqrt(moment_two) + epsilon)).astype(jnp.bfloat16)
    direction = lax.optimization_barrier(direction).astype(jnp.float32).reshape(SEQS, D * ADAPTER_RANK)
    seed_values = jnp.repeat(block_seeds, FEAT_BLOCK)
    feature_index = jnp.arange(K, dtype=jnp.int32)
    param_block = math.gcd(D * ADAPTER_RANK, 8192)

    def accumulate(block_number, running):
        start_param = (block_number * param_block).astype(jnp.int32)
        param_index = start_param + jnp.arange(param_block, dtype=jnp.int32)
        sign_tile = sign_block(seed_values, feature_index, param_index).astype(jnp.float32)
        direction_piece = lax.dynamic_slice_in_dim(direction, start_param, param_block, 1)
        return running + lax.dot_general(direction_piece, sign_tile, (((1,), (1,)), ((), ())), precision=lax.Precision.HIGHEST, preferred_element_type=jnp.float32)
    features = lax.fori_loop(jnp.int32(0), jnp.int32(D * ADAPTER_RANK // param_block), accumulate, jnp.zeros((SEQS, K), jnp.float32))
    features = features * (1.0 / math.sqrt(D * ADAPTER_RANK))
    return features.reshape(SEQS * 2, K // 2)
```

```python
import functools
import math

import jax
import jax.numpy as jnp
from jax import lax
from jax.experimental import pallas as pl
from jax.experimental.pallas import tpu as pltpu
from jax.sharding import PartitionSpec as P

FEAT_BLOCK = 512


beta_one = 0.9
beta_two = 0.999
epsilon = 1e-08
mix_feature = 1640531527
mix_param = 2028178513
mix_round = 73244475

GRAD_COLUMNS = 1024
TILE_ROWS = 4
STRIP = 32


def wrapped(number):
    number %= 2**32
    return number - 2**32 if number >= 2**31 else number


def grad_kernel(shape, side_ref, hidden_ref, masked_ref, *out_refs):
    local_rows, groups, half, piece = shape
    chunks = half // piece
    product = lax.dot_general(
        hidden_ref[...],
        masked_ref[...],
        (((0,), (0,)), ((), ())),
        preferred_element_type=jnp.float32,
    )
    first = side_ref[0] == 0
    for owner in range(product.shape[0] // local_rows):
        for group in range(groups):
            start = owner * local_rows + group * 2 * half
            for chunk in range(chunks):
                low = start + chunk * piece
                low_rows = product[low : low + piece]
                high_rows = product[low + half : low + half + piece]
                out_refs[chunk][group, owner] = jnp.where(first, low_rows, high_rows)
                out_refs[chunks + chunk][group, owner] = jnp.where(first, high_rows, low_rows)


def half_gradients(hidden, masked, side, device_list, groups, half, piece):
    tokens, width = hidden.shape
    rank = masked.shape[1]
    local_rows = width // device_list
    chunks = half // piece
    owners = GRAD_COLUMNS // local_rows
    block = pl.BlockSpec((groups, owners, piece, rank), lambda step: (0, step, 0, 0))
    return pl.pallas_call(
        functools.partial(grad_kernel, (local_rows, groups, half, piece)),
        grid=(width // GRAD_COLUMNS,),
        in_specs=[
            pl.BlockSpec(memory_space=pltpu.SMEM),
            pl.BlockSpec((tokens, GRAD_COLUMNS), lambda step: (0, step)),
            pl.BlockSpec((tokens, rank), lambda step: (0, 0)),
        ],
        out_specs=[block] * (2 * chunks),
        out_shape=[jax.ShapeDtypeStruct((groups, device_list, piece, rank), jnp.float32)] * (2 * chunks),
        compiler_params=pltpu.CompilerParams(vmem_limit_bytes=32 * 2**20),
        cost_estimate=pl.CostEstimate(
            flops=2 * tokens * width * rank, bytes_accessed=2 * tokens * width + 4 * width * rank, transcendentals=0
        ),
    )(side, hidden, masked)


def sign_strip(hashed):
    hashed = hashed ^ lax.shift_right_logical(hashed, jnp.full_like(hashed, 16))
    hashed = hashed * mix_round
    hashed = hashed ^ lax.shift_right_logical(hashed, jnp.full_like(hashed, 16))
    hashed = hashed * mix_round
    return jnp.where(hashed < 0, -1.0, 1.0).astype(jnp.bfloat16)


def project_kernel(
    shape, place_ref, seeds_ref, grad_ref, one_ref, two_ref, before_ref, out_ref,
    directions, base, tile_a, tile_b, total,
):
    sequences, piece, half, rank, scale = shape
    block_number = pl.program_id(0)
    rows = 2 * piece
    tiles = rows // TILE_ROWS

    @pl.when(block_number == 0)
    def _():
        for side in range(2):
            def prepare(row, carry, side=side):
                gradient = grad_ref[pl.ds(side * piece + row, sequences, stride=rows), :]
                at = pl.ds(place_ref[0] + side * half + row, 1)
                moment_one = beta_one * one_ref[at, :] + (1 - beta_one) * gradient
                moment_two = beta_two * two_ref[at, :] + (1 - beta_two) * gradient * gradient
                direction = moment_one / (jnp.sqrt(moment_two) + epsilon)
                directions[side * piece + row] = direction.astype(jnp.bfloat16)
                return carry

            lax.fori_loop(0, piece, prepare, 0)

    feature = block_number * FEAT_BLOCK + lax.broadcasted_iota(jnp.int32, base.shape, 0)
    column = lax.broadcasted_iota(jnp.int32, base.shape, 1)
    base[...] = seeds_ref[block_number] + feature * mix_feature + column * mix_param
    total[...] = jnp.zeros_like(total)
    row_step = jnp.int32(wrapped(mix_param * rank))

    def fill(tile, held):
        row = tile * TILE_ROWS
        side = row // piece
        first = place_ref[1] + side * half + (row - side * piece)
        for step in range(TILE_ROWS):
            offset = (first + step) * row_step
            for strip in range(0, FEAT_BLOCK, STRIP):
                held[strip : strip + STRIP, step * rank : (step + 1) * rank] = sign_strip(
                    base[strip : strip + STRIP, :] + offset
                )

    def add(tile, held):
        weights = jnp.concatenate(
            [directions[tile * TILE_ROWS + step] for step in range(TILE_ROWS)], axis=1
        )
        total[...] += lax.dot_general(
            held[...], weights, (((1,), (1,)), ((), ())), preferred_element_type=jnp.float32
        )

    fill(0, tile_a)

    def pair(index, carry):
        add(2 * index, tile_a)
        fill(2 * index + 1, tile_b)
        add(2 * index + 1, tile_b)
        fill(2 * index + 2, tile_a)
        return carry

    lax.fori_loop(0, tiles // 2 - 1, pair, 0)
    add(tiles - 2, tile_a)
    fill(tiles - 1, tile_b)
    add(tiles - 1, tile_b)
    out_ref[...] = before_ref[...] + total[...].T * scale


def project(place, seeds, received, moment_one, moment_two, before, sequences, piece, half, scale):
    rank = received.shape[1]
    features = seeds.shape[0] * FEAT_BLOCK
    rows = 2 * piece
    whole = lambda array: pl.BlockSpec(array.shape, lambda block: (0, 0))
    part = pl.BlockSpec((sequences, FEAT_BLOCK), lambda block: (0, block))
    return pl.pallas_call(
        functools.partial(project_kernel, (sequences, piece, half, rank, scale)),
        grid=(seeds.shape[0],),
        in_specs=[
            pl.BlockSpec(memory_space=pltpu.SMEM),
            pl.BlockSpec(memory_space=pltpu.SMEM),
            whole(received),
            whole(moment_one),
            whole(moment_two),
            part,
        ],
        out_specs=part,
        out_shape=jax.ShapeDtypeStruct((sequences, features), jnp.float32),
        scratch_shapes=[
            pltpu.VMEM((rows, sequences, rank), jnp.bfloat16),
            pltpu.VMEM((FEAT_BLOCK, rank), jnp.int32),
            pltpu.VMEM((FEAT_BLOCK, TILE_ROWS * rank), jnp.bfloat16),
            pltpu.VMEM((FEAT_BLOCK, TILE_ROWS * rank), jnp.bfloat16),
            pltpu.VMEM((FEAT_BLOCK, sequences), jnp.float32),
        ],
        compiler_params=pltpu.CompilerParams(vmem_limit_bytes=32 * 2**20),
        cost_estimate=pl.CostEstimate(
            flops=400 * rows * rank * features, bytes_accessed=4 * received.size, transcendentals=0
        ),
    )(place, seeds, received, moment_one, moment_two, before)


def local(
    hidden_input_rows,
    rank_cotangent,
    token_identifiers,
    adam_first_moment,
    adam_second_moment,
    block_seeds,
):
    axes = ("groups", "dp")
    groups = lax.axis_size("groups")
    device_list = lax.axis_size("dp")
    my_group = lax.axis_index("groups")
    my_index = lax.axis_index("dp")
    hidden_width = hidden_input_rows.shape[1]
    rank = rank_cotangent.shape[1]
    local_rows = adam_first_moment.shape[0]
    owned = local_rows // groups
    half = owned // 2
    piece = max(8, half // 4)
    devices = groups * device_list
    sequences = devices // 2
    scale = 1.0 / math.sqrt(hidden_width * rank)

    padding_mask = (token_identifiers != 0).astype(jnp.bfloat16)
    masked_values = rank_cotangent * padding_mask[:, None]
    side = jnp.reshape(my_index % 2, (1,)).astype(jnp.int32)
    blocks = half_gradients(hidden_input_rows, masked_values, side, device_list, groups, half, piece)
    chunks = half // piece
    pairs = [(source, source ^ 1) for source in range(device_list)]
    received = []
    for chunk in range(chunks):
        other = lax.ppermute(blocks[chunks + chunk], "dp", pairs)
        summed = (blocks[chunk] + other).reshape(devices, piece, rank)
        gathered = lax.all_to_all(summed, axes, split_axis=0, concat_axis=0, tiled=True)
        received.append(gathered.reshape(devices * piece, rank))

    partials = jnp.zeros((sequences, block_seeds.shape[0] * FEAT_BLOCK), jnp.float32)
    for chunk in range(chunks):
        in_slice = my_group * owned + chunk * piece
        place = jnp.stack([in_slice, my_index * local_rows + in_slice]).astype(jnp.int32)
        partials = project(
            place, block_seeds, received[chunk], adam_first_moment, adam_second_moment, partials,
            sequences, piece, half, scale,
        )
    shares = partials.reshape(devices, -1)
    shares = lax.all_to_all(shares, axes, split_axis=0, concat_axis=0, tiled=True)
    return jnp.sum(shares, axis=0, keepdims=True)


def solution(mesh):
    in_specs = (
        P(("groups", "dp"), None),
        P(("groups", "dp"), None),
        P(("groups", "dp")),
        P("dp", None),
        P("dp", None),
        P(),
    )
    out_specs = P(("groups", "dp"), None)
    return jax.shard_map(local, mesh=mesh, in_specs=in_specs, out_specs=out_specs, check_vma=False)
```

```python
import functools
import math

import jax
import jax.numpy as jnp
from jax import lax
from jax.experimental import pallas as pl
from jax.experimental.pallas import tpu as pltpu
from jax.sharding import PartitionSpec as P

FEAT_BLOCK = 512


beta_one = 0.9
beta_two = 0.999
epsilon = 1e-08
mix_feature = 1640531527
mix_param = 2028178513
mix_round = 73244475

GRAD_COLUMNS = 1024
TILE_ROWS = 4
STRIP = 16


def wrapped(number):
    number %= 2**32
    return number - 2**32 if number >= 2**31 else number


def grad_kernel(shape, side_ref, hidden_ref, masked_ref, *out_refs):
    local_rows, groups, half, pieces = shape
    chunks = len(pieces)
    product = lax.dot_general(
        hidden_ref[...],
        masked_ref[...],
        (((0,), (0,)), ((), ())),
        preferred_element_type=jnp.float32,
    )
    first = side_ref[0] == 0
    for owner in range(product.shape[0] // local_rows):
        for group in range(groups):
            start = owner * local_rows + group * 2 * half
            for chunk, (offset, piece) in enumerate(pieces):
                low = start + offset
                low_rows = product[low : low + piece]
                high_rows = product[low + half : low + half + piece]
                out_refs[chunk][group, owner] = jnp.where(first, low_rows, high_rows)
                out_refs[chunks + chunk][group, owner] = jnp.where(first, high_rows, low_rows)


def half_gradients(hidden, masked, side, device_list, groups, half, pieces):
    tokens, width = hidden.shape
    rank = masked.shape[1]
    local_rows = width // device_list
    sizes = [piece for _, piece in pieces] * 2
    owners = GRAD_COLUMNS // local_rows
    return pl.pallas_call(
        functools.partial(grad_kernel, (local_rows, groups, half, pieces)),
        grid=(width // GRAD_COLUMNS,),
        in_specs=[
            pl.BlockSpec(memory_space=pltpu.SMEM),
            pl.BlockSpec((tokens, GRAD_COLUMNS), lambda step: (0, step)),
            pl.BlockSpec((tokens, rank), lambda step: (0, 0)),
        ],
        out_specs=[
            pl.BlockSpec((groups, owners, size, rank), lambda step: (0, step, 0, 0)) for size in sizes
        ],
        out_shape=[
            jax.ShapeDtypeStruct((groups, device_list, size, rank), jnp.float32) for size in sizes
        ],
        compiler_params=pltpu.CompilerParams(vmem_limit_bytes=32 * 2**20),
        cost_estimate=pl.CostEstimate(
            flops=2 * tokens * width * rank, bytes_accessed=2 * tokens * width + 4 * width * rank, transcendentals=0
        ),
    )(side, hidden, masked)


def sign_strip(hashed):
    hashed = hashed ^ lax.shift_right_logical(hashed, jnp.full_like(hashed, 16))
    hashed = hashed * mix_round
    hashed = hashed ^ lax.shift_right_logical(hashed, jnp.full_like(hashed, 16))
    hashed = hashed * mix_round
    return jnp.where(hashed < 0, -1.0, 1.0).astype(jnp.bfloat16)


def project_kernel(
    shape, place_ref, seeds_ref, grad_ref, one_ref, two_ref, before_ref, out_ref,
    directions, base, tile_a, tile_b, total,
):
    sequences, piece, half, rank, scale = shape
    block_number = pl.program_id(0)
    rows = 2 * piece
    tiles = rows // TILE_ROWS

    @pl.when(block_number == 0)
    def _():
        for side in range(2):
            def prepare(row, carry, side=side):
                gradient = grad_ref[pl.ds(side * piece + row, sequences, stride=rows), :]
                at = pl.ds(place_ref[0] + side * half + row, 1)
                moment_one = beta_one * one_ref[at, :] + (1 - beta_one) * gradient
                moment_two = beta_two * two_ref[at, :] + (1 - beta_two) * gradient * gradient
                direction = moment_one / (jnp.sqrt(moment_two) + epsilon)
                directions[side * piece + row] = direction.astype(jnp.bfloat16)
                return carry

            lax.fori_loop(0, piece, prepare, 0)

    column = lax.broadcasted_iota(jnp.int32, base.shape, 0)
    feature = block_number * FEAT_BLOCK + lax.broadcasted_iota(jnp.int32, base.shape, 1)
    base[...] = seeds_ref[block_number] + feature * mix_feature + column * mix_param
    total[...] = jnp.zeros_like(total)
    row_step = jnp.int32(wrapped(mix_param * rank))

    def fill(tile, held):
        row = tile * TILE_ROWS
        side = row // piece
        first = place_ref[1] + side * half + (row - side * piece)
        for step in range(TILE_ROWS):
            offset = (first + step) * row_step
            for strip in range(0, rank, STRIP):
                at = step * rank + strip
                held[at : at + STRIP, :] = sign_strip(base[strip : strip + STRIP, :] + offset)

    def add(tile, held):
        directed = jnp.concatenate(
            [directions[tile * TILE_ROWS + step] for step in range(TILE_ROWS)], axis=1
        )
        total[...] += jnp.dot(directed, held[...], preferred_element_type=jnp.float32)

    fill(0, tile_a)

    def pair(index, carry):
        add(2 * index, tile_a)
        fill(2 * index + 1, tile_b)
        add(2 * index + 1, tile_b)
        fill(2 * index + 2, tile_a)
        return carry

    lax.fori_loop(0, tiles // 2 - 1, pair, 0)
    add(tiles - 2, tile_a)
    fill(tiles - 1, tile_b)
    add(tiles - 1, tile_b)
    out_ref[...] = before_ref[...] + total[...] * scale


def project(place, seeds, received, moment_one, moment_two, before, sequences, piece, half, scale):
    rank = received.shape[1]
    features = seeds.shape[0] * FEAT_BLOCK
    rows = 2 * piece
    whole = lambda array: pl.BlockSpec(array.shape, lambda block: (0, 0))
    part = pl.BlockSpec((sequences, FEAT_BLOCK), lambda block: (0, block))
    return pl.pallas_call(
        functools.partial(project_kernel, (sequences, piece, half, rank, scale)),
        grid=(seeds.shape[0],),
        in_specs=[
            pl.BlockSpec(memory_space=pltpu.SMEM),
            pl.BlockSpec(memory_space=pltpu.SMEM),
            whole(received),
            whole(moment_one),
            whole(moment_two),
            part,
        ],
        out_specs=part,
        out_shape=jax.ShapeDtypeStruct((sequences, features), jnp.float32),
        scratch_shapes=[
            pltpu.VMEM((rows, sequences, rank), jnp.bfloat16),
            pltpu.VMEM((rank, FEAT_BLOCK), jnp.int32),
            pltpu.VMEM((TILE_ROWS * rank, FEAT_BLOCK), jnp.bfloat16),
            pltpu.VMEM((TILE_ROWS * rank, FEAT_BLOCK), jnp.bfloat16),
            pltpu.VMEM((sequences, FEAT_BLOCK), jnp.float32),
        ],
        compiler_params=pltpu.CompilerParams(vmem_limit_bytes=32 * 2**20),
        cost_estimate=pl.CostEstimate(
            flops=400 * rows * rank * features, bytes_accessed=4 * received.size, transcendentals=0
        ),
    )(place, seeds, received, moment_one, moment_two, before)


def local(
    hidden_input_rows,
    rank_cotangent,
    token_identifiers,
    adam_first_moment,
    adam_second_moment,
    block_seeds,
):
    axes = ("groups", "dp")
    groups = lax.axis_size("groups")
    device_list = lax.axis_size("dp")
    my_group = lax.axis_index("groups")
    my_index = lax.axis_index("dp")
    hidden_width = hidden_input_rows.shape[1]
    rank = rank_cotangent.shape[1]
    local_rows = adam_first_moment.shape[0]
    owned = local_rows // groups
    half = owned // 2
    first = max(8, half // 4)
    pieces = ((0, first), (first, half - first))
    devices = groups * device_list
    sequences = devices // 2
    scale = 1.0 / math.sqrt(hidden_width * rank)

    padding_mask = (token_identifiers != 0).astype(jnp.bfloat16)
    masked_values = rank_cotangent * padding_mask[:, None]
    side = jnp.reshape(my_index % 2, (1,)).astype(jnp.int32)
    blocks = half_gradients(hidden_input_rows, masked_values, side, device_list, groups, half, pieces)
    chunks = len(pieces)
    pairs = [(source, source ^ 1) for source in range(device_list)]
    received = []
    for chunk, (_, piece) in enumerate(pieces):
        other = lax.ppermute(blocks[chunks + chunk], "dp", pairs)
        summed = (blocks[chunk] + other).reshape(devices, piece, rank)
        gathered = lax.all_to_all(summed, axes, split_axis=0, concat_axis=0, tiled=True)
        received.append(gathered.reshape(devices * piece, rank))

    partials = jnp.zeros((sequences, block_seeds.shape[0] * FEAT_BLOCK), jnp.float32)
    for chunk, (offset, piece) in enumerate(pieces):
        in_slice = my_group * owned + offset
        place = jnp.stack([in_slice, my_index * local_rows + in_slice]).astype(jnp.int32)
        partials = project(
            place, block_seeds, received[chunk], adam_first_moment, adam_second_moment, partials,
            sequences, piece, half, scale,
        )
    shares = partials.reshape(devices, -1)
    shares = lax.all_to_all(shares, axes, split_axis=0, concat_axis=0, tiled=True)
    return jnp.sum(shares, axis=0, keepdims=True)


def solution(mesh):
    in_specs = (
        P(("groups", "dp"), None),
        P(("groups", "dp"), None),
        P(("groups", "dp")),
        P("dp", None),
        P("dp", None),
        P(),
    )
    out_specs = P(("groups", "dp"), None)
    return jax.shard_map(local, mesh=mesh, in_specs=in_specs, out_specs=out_specs, check_vma=False)
```

```python
import functools
import math

import jax
import jax.numpy as jnp
from jax import lax
from jax.experimental import pallas as pl
from jax.experimental.pallas import tpu as pltpu
from jax.sharding import PartitionSpec as P

FEAT_BLOCK = 512


beta_one = 0.9
beta_two = 0.999
epsilon = 1e-08
mix_feature = 1640531527
mix_param = 2028178513
mix_round = 73244475

GRAD_COLUMNS = 1024
TILE_ROWS = 2
STRIP = 16
PASS_COLUMNS = 256


def wrapped(number):
    number %= 2**32
    return number - 2**32 if number >= 2**31 else number


def grad_kernel(shape, side_ref, hidden_ref, masked_ref, *out_refs):
    local_rows, groups, half, pieces = shape
    chunks = len(pieces)
    product = lax.dot_general(
        hidden_ref[...],
        masked_ref[...],
        (((0,), (0,)), ((), ())),
        preferred_element_type=jnp.float32,
    )
    first = side_ref[0] == 0
    for owner in range(product.shape[0] // local_rows):
        for group in range(groups):
            start = owner * local_rows + group * 2 * half
            for chunk, (offset, piece) in enumerate(pieces):
                low = start + offset
                low_rows = product[low : low + piece]
                high_rows = product[low + half : low + half + piece]
                out_refs[chunk][group, owner] = jnp.where(first, low_rows, high_rows)
                out_refs[chunks + chunk][group, owner] = jnp.where(first, high_rows, low_rows)


def half_gradients(hidden, masked, side, device_list, groups, half, pieces):
    tokens, width = hidden.shape
    rank = masked.shape[1]
    local_rows = width // device_list
    sizes = [piece for _, piece in pieces] * 2
    owners = GRAD_COLUMNS // local_rows
    return pl.pallas_call(
        functools.partial(grad_kernel, (local_rows, groups, half, pieces)),
        grid=(width // GRAD_COLUMNS,),
        in_specs=[
            pl.BlockSpec(memory_space=pltpu.SMEM),
            pl.BlockSpec((tokens, GRAD_COLUMNS), lambda step: (0, step)),
            pl.BlockSpec((tokens, rank), lambda step: (0, 0)),
        ],
        out_specs=[
            pl.BlockSpec((groups, owners, size, rank), lambda step: (0, step, 0, 0)) for size in sizes
        ],
        out_shape=[
            jax.ShapeDtypeStruct((groups, device_list, size, rank), jnp.float32) for size in sizes
        ],
        compiler_params=pltpu.CompilerParams(vmem_limit_bytes=32 * 2**20),
        cost_estimate=pl.CostEstimate(
            flops=2 * tokens * width * rank, bytes_accessed=2 * tokens * width + 4 * width * rank, transcendentals=0
        ),
    )(side, hidden, masked)


def sign_strip(hashed):
    hashed = hashed ^ lax.shift_right_logical(hashed, jnp.full_like(hashed, 16))
    hashed = hashed * mix_round
    hashed = hashed ^ lax.shift_right_logical(hashed, jnp.full_like(hashed, 16))
    hashed = hashed * mix_round
    return jnp.where(hashed < 0, -1.0, 1.0).astype(jnp.bfloat16)


def project_kernel(
    shape, place_ref, seeds_ref, grad_ref, one_ref, two_ref, before_ref, out_ref,
    directions, base, tile_a, tile_b, total,
):
    sequences, piece, half, rank, scale = shape
    block_number = pl.program_id(0)
    rows = 2 * piece
    tiles = rows // TILE_ROWS

    @pl.when(block_number == 0)
    def _():
        for side in range(2):
            def prepare(row, carry, side=side):
                gradient = grad_ref[pl.ds(side * piece + row, sequences, stride=rows), :]
                at = pl.ds(place_ref[0] + side * half + row, 1)
                moment_one = beta_one * one_ref[at, :] + (1 - beta_one) * gradient
                moment_two = beta_two * two_ref[at, :] + (1 - beta_two) * gradient * gradient
                direction = moment_one / (jnp.sqrt(moment_two) + epsilon)
                directions[side * piece + row] = direction.astype(jnp.bfloat16)
                return carry

            lax.fori_loop(0, piece, prepare, 0)

    column = lax.broadcasted_iota(jnp.int32, base.shape, 0)
    feature = block_number * FEAT_BLOCK + lax.broadcasted_iota(jnp.int32, base.shape, 1)
    base[...] = seeds_ref[block_number] + feature * mix_feature + column * mix_param
    total[...] = jnp.zeros_like(total)
    row_step = jnp.int32(wrapped(mix_param * rank))

    passes = FEAT_BLOCK // PASS_COLUMNS
    strips = [
        (step, strip) for step in range(TILE_ROWS) for strip in range(0, rank, STRIP)
    ]

    def fill(tile, held, part):
        row = tile * TILE_ROWS
        side = row // piece
        first = place_ref[1] + side * half + (row - side * piece)
        for step, strip in strips[part * len(strips) // passes : (part + 1) * len(strips) // passes]:
            at = step * rank + strip
            offset = (first + step) * row_step
            held[at : at + STRIP, :] = sign_strip(base[strip : strip + STRIP, :] + offset)

    def add(tile, held, part):
        directed = jnp.concatenate(
            [directions[tile * TILE_ROWS + step] for step in range(TILE_ROWS)], axis=1
        )
        columns = pl.ds(part * PASS_COLUMNS, PASS_COLUMNS)
        total[:, columns] += jnp.dot(directed, held[:, columns], preferred_element_type=jnp.float32)

    def both(tile, held, other):
        for part in range(passes):
            add(tile, held, part)
            fill(tile + 1, other, part)

    for part in range(passes):
        fill(0, tile_a, part)

    def pair(index, carry):
        both(2 * index, tile_a, tile_b)
        both(2 * index + 1, tile_b, tile_a)
        return carry

    lax.fori_loop(0, tiles // 2 - 1, pair, 0)
    both(tiles - 2, tile_a, tile_b)
    for part in range(passes):
        add(tiles - 1, tile_b, part)
    out_ref[...] = before_ref[...] + total[...] * scale


def project(place, seeds, received, moment_one, moment_two, before, sequences, piece, half, scale):
    rank = received.shape[1]
    features = seeds.shape[0] * FEAT_BLOCK
    rows = 2 * piece
    whole = lambda array: pl.BlockSpec(array.shape, lambda block: (0, 0))
    part = pl.BlockSpec((sequences, FEAT_BLOCK), lambda block: (0, block))
    return pl.pallas_call(
        functools.partial(project_kernel, (sequences, piece, half, rank, scale)),
        grid=(seeds.shape[0],),
        in_specs=[
            pl.BlockSpec(memory_space=pltpu.SMEM),
            pl.BlockSpec(memory_space=pltpu.SMEM),
            whole(received),
            whole(moment_one),
            whole(moment_two),
            part,
        ],
        out_specs=part,
        out_shape=jax.ShapeDtypeStruct((sequences, features), jnp.float32),
        scratch_shapes=[
            pltpu.VMEM((rows, sequences, rank), jnp.bfloat16),
            pltpu.VMEM((rank, FEAT_BLOCK), jnp.int32),
            pltpu.VMEM((TILE_ROWS * rank, FEAT_BLOCK), jnp.bfloat16),
            pltpu.VMEM((TILE_ROWS * rank, FEAT_BLOCK), jnp.bfloat16),
            pltpu.VMEM((sequences, FEAT_BLOCK), jnp.float32),
        ],
        compiler_params=pltpu.CompilerParams(vmem_limit_bytes=32 * 2**20),
        cost_estimate=pl.CostEstimate(
            flops=400 * rows * rank * features, bytes_accessed=4 * received.size, transcendentals=0
        ),
    )(place, seeds, received, moment_one, moment_two, before)


def gather_kernel(groups, device_list, shares_ref, out_ref, landing, send_sem, recv_sem):
    devices = groups * device_list
    me = lax.axis_index("groups") * device_list + lax.axis_index("dp")

    def place(offset):
        target = lax.rem(me + offset, devices)
        return target, (target // device_list, lax.rem(target, device_list))

    barrier = pltpu.get_barrier_semaphore()

    def greet(offset, carry):
        pl.semaphore_signal(barrier, inc=1, device_id=place(offset)[1], device_id_type=pl.DeviceIdType.MESH)
        return carry

    lax.fori_loop(1, devices, greet, 0)
    pl.semaphore_wait(barrier, devices - 1)

    def send(offset, carry):
        target, where = place(offset)
        pltpu.make_async_remote_copy(
            src_ref=shares_ref.at[target],
            dst_ref=landing.at[offset - 1],
            send_sem=send_sem,
            recv_sem=recv_sem,
            device_id=where,
            device_id_type=pl.DeviceIdType.MESH,
        ).start()
        return carry

    lax.fori_loop(1, devices, send, 0)
    pltpu.make_async_copy(landing, landing, recv_sem).wait()
    out_ref[...] = shares_ref[me] + jnp.sum(landing[...], axis=0)
    pltpu.make_async_copy(landing, landing, send_sem).wait()


def sum_shares(shares, groups, device_list):
    devices, rows, columns = shares.shape
    vmem = pl.BlockSpec(memory_space=pltpu.VMEM)
    return pl.pallas_call(
        functools.partial(gather_kernel, groups, device_list),
        in_specs=[vmem],
        out_specs=vmem,
        out_shape=jax.ShapeDtypeStruct((rows, columns), jnp.float32),
        scratch_shapes=[
            pltpu.VMEM((devices - 1, rows, columns), jnp.float32),
            pltpu.SemaphoreType.DMA,
            pltpu.SemaphoreType.DMA,
        ],
        compiler_params=pltpu.CompilerParams(
            collective_id=0, has_side_effects=True, vmem_limit_bytes=32 * 2**20
        ),
        cost_estimate=pl.CostEstimate(flops=shares.size, bytes_accessed=8 * shares.size, transcendentals=0),
    )(shares)


def local(
    hidden_input_rows,
    rank_cotangent,
    token_identifiers,
    adam_first_moment,
    adam_second_moment,
    block_seeds,
):
    axes = ("groups", "dp")
    groups = lax.axis_size("groups")
    device_list = lax.axis_size("dp")
    my_group = lax.axis_index("groups")
    my_index = lax.axis_index("dp")
    hidden_width = hidden_input_rows.shape[1]
    rank = rank_cotangent.shape[1]
    local_rows = adam_first_moment.shape[0]
    owned = local_rows // groups
    half = owned // 2
    first = max(8, half // 4)
    pieces = ((0, first), (first, half - first))
    devices = groups * device_list
    sequences = devices // 2
    scale = 1.0 / math.sqrt(hidden_width * rank)

    padding_mask = (token_identifiers != 0).astype(jnp.bfloat16)
    masked_values = rank_cotangent * padding_mask[:, None]
    side = jnp.reshape(my_index % 2, (1,)).astype(jnp.int32)
    blocks = half_gradients(hidden_input_rows, masked_values, side, device_list, groups, half, pieces)
    chunks = len(pieces)
    pairs = [(source, source ^ 1) for source in range(device_list)]
    received = []
    for chunk, (_, piece) in enumerate(pieces):
        other = lax.ppermute(blocks[chunks + chunk], "dp", pairs)
        summed = (blocks[chunk] + other).reshape(devices, piece, rank)
        gathered = lax.all_to_all(summed, axes, split_axis=0, concat_axis=0, tiled=True)
        received.append(gathered.reshape(devices * piece, rank))

    partials = jnp.zeros((sequences, block_seeds.shape[0] * FEAT_BLOCK), jnp.float32)
    for chunk, (offset, piece) in enumerate(pieces):
        in_slice = my_group * owned + offset
        place = jnp.stack([in_slice, my_index * local_rows + in_slice]).astype(jnp.int32)
        partials = project(
            place, block_seeds, received[chunk], adam_first_moment, adam_second_moment, partials,
            sequences, piece, half, scale,
        )
    shares = partials.reshape(devices, 8, -1)
    return sum_shares(shares, groups, device_list).reshape(1, -1)


def solution(mesh):
    in_specs = (
        P(("groups", "dp"), None),
        P(("groups", "dp"), None),
        P(("groups", "dp")),
        P("dp", None),
        P("dp", None),
        P(),
    )
    out_specs = P(("groups", "dp"), None)
    return jax.shard_map(local, mesh=mesh, in_specs=in_specs, out_specs=out_specs, check_vma=False)
```

```python
import functools
import math

import jax
import jax.numpy as jnp
from jax import lax
from jax.experimental import pallas as pl
from jax.experimental.pallas import tpu as pltpu
from jax.sharding import PartitionSpec as P

FEAT_BLOCK = 512


beta_one = 0.9
beta_two = 0.999
epsilon = 1e-08
mix_feature = 1640531527
mix_param = 2028178513
mix_round = 73244475

GRAD_COLUMNS = 1024
TILE_ROWS = 2
BODY_ROWS = 16
STRIP = 32
PASS_COLUMNS = 256


def wrapped(number):
    number %= 2**32
    return number - 2**32 if number >= 2**31 else number


def grad_kernel(shape, side_ref, hidden_ref, masked_ref, *out_refs):
    local_rows, groups, half, pieces = shape
    chunks = len(pieces)
    product = lax.dot_general(
        hidden_ref[...],
        masked_ref[...],
        (((0,), (0,)), ((), ())),
        preferred_element_type=jnp.float32,
    )
    first = side_ref[0] == 0
    for owner in range(product.shape[0] // local_rows):
        for group in range(groups):
            start = owner * local_rows + group * 2 * half
            for chunk, (offset, piece) in enumerate(pieces):
                low = start + offset
                low_rows = product[low : low + piece]
                high_rows = product[low + half : low + half + piece]
                out_refs[chunk][group, owner] = jnp.where(first, low_rows, high_rows)
                out_refs[chunks + chunk][group, owner] = jnp.where(first, high_rows, low_rows)


def half_gradients(hidden, masked, side, device_list, groups, half, pieces):
    tokens, width = hidden.shape
    rank = masked.shape[1]
    local_rows = width // device_list
    sizes = [piece for _, piece in pieces] * 2
    owners = GRAD_COLUMNS // local_rows
    return pl.pallas_call(
        functools.partial(grad_kernel, (local_rows, groups, half, pieces)),
        grid=(width // GRAD_COLUMNS,),
        in_specs=[
            pl.BlockSpec(memory_space=pltpu.SMEM),
            pl.BlockSpec((tokens, GRAD_COLUMNS), lambda step: (0, step)),
            pl.BlockSpec((tokens, rank), lambda step: (0, 0)),
        ],
        out_specs=[
            pl.BlockSpec((groups, owners, size, rank), lambda step: (0, step, 0, 0)) for size in sizes
        ],
        out_shape=[
            jax.ShapeDtypeStruct((groups, device_list, size, rank), jnp.float32) for size in sizes
        ],
        compiler_params=pltpu.CompilerParams(vmem_limit_bytes=32 * 2**20),
        cost_estimate=pl.CostEstimate(
            flops=2 * tokens * width * rank, bytes_accessed=2 * tokens * width + 4 * width * rank, transcendentals=0
        ),
    )(side, hidden, masked)


def sign_strip(hashed):
    hashed = hashed ^ lax.shift_right_logical(hashed, jnp.full_like(hashed, 16))
    hashed = hashed * mix_round
    hashed = hashed ^ lax.shift_right_logical(hashed, jnp.full_like(hashed, 16))
    hashed = hashed * mix_round
    return jnp.where(hashed < 0, -1.0, 1.0).astype(jnp.bfloat16)


def project_kernel(
    shape, place_ref, seeds_ref, grad_ref, one_ref, two_ref, before_ref, out_ref,
    directions, base,
):
    sequences, piece, half, rank, scale = shape
    block_number = pl.program_id(0)
    rows = 2 * piece

    @pl.when(block_number == 0)
    def _():
        for side in range(2):
            def prepare(row, carry, side=side):
                gradient = grad_ref[pl.ds(side * piece + row, sequences, stride=rows), :]
                at = pl.ds(place_ref[0] + side * half + row, 1)
                moment_one = beta_one * one_ref[at, :] + (1 - beta_one) * gradient
                moment_two = beta_two * two_ref[at, :] + (1 - beta_two) * gradient * gradient
                direction = moment_one / (jnp.sqrt(moment_two) + epsilon)
                directions[side * piece + row] = direction.astype(jnp.bfloat16)
                return carry

            lax.fori_loop(0, piece, prepare, 0)

    column = lax.broadcasted_iota(jnp.int32, base.shape, 0)
    feature = block_number * FEAT_BLOCK + lax.broadcasted_iota(jnp.int32, base.shape, 1)
    base[...] = seeds_ref[block_number] + feature * mix_feature + column * mix_param
    row_step = jnp.int32(wrapped(mix_param * rank))

    passes = FEAT_BLOCK // PASS_COLUMNS

    def body(index, sums):
        sums = list(sums)
        for tile in range(BODY_ROWS // TILE_ROWS):
            row = index * BODY_ROWS + tile * TILE_ROWS
            side = row // piece
            first = place_ref[1] + side * half + (row - side * piece)
            directed = jnp.concatenate(
                [directions[row + step] for step in range(TILE_ROWS)], axis=1
            )
            for part in range(passes):
                columns = slice(part * PASS_COLUMNS, (part + 1) * PASS_COLUMNS)
                signs = jnp.concatenate(
                    [
                        sign_strip(base[strip : strip + STRIP, columns] + (first + step) * row_step)
                        for step in range(TILE_ROWS)
                        for strip in range(0, rank, STRIP)
                    ],
                    axis=0,
                )
                sums[part] += jnp.dot(directed, signs, preferred_element_type=jnp.float32)
        return tuple(sums)

    zero = jnp.zeros((sequences, PASS_COLUMNS), jnp.float32)
    sums = lax.fori_loop(0, rows // BODY_ROWS, body, (zero,) * passes)
    out_ref[...] = before_ref[...] + jnp.concatenate(sums, axis=1) * scale


def project(place, seeds, received, moment_one, moment_two, before, sequences, piece, half, scale):
    rank = received.shape[1]
    features = seeds.shape[0] * FEAT_BLOCK
    rows = 2 * piece
    whole = lambda array: pl.BlockSpec(array.shape, lambda block: (0, 0))
    part = pl.BlockSpec((sequences, FEAT_BLOCK), lambda block: (0, block))
    return pl.pallas_call(
        functools.partial(project_kernel, (sequences, piece, half, rank, scale)),
        grid=(seeds.shape[0],),
        in_specs=[
            pl.BlockSpec(memory_space=pltpu.SMEM),
            pl.BlockSpec(memory_space=pltpu.SMEM),
            whole(received),
            whole(moment_one),
            whole(moment_two),
            part,
        ],
        out_specs=part,
        out_shape=jax.ShapeDtypeStruct((sequences, features), jnp.float32),
        scratch_shapes=[
            pltpu.VMEM((rows, sequences, rank), jnp.bfloat16),
            pltpu.VMEM((rank, FEAT_BLOCK), jnp.int32),
        ],
        compiler_params=pltpu.CompilerParams(vmem_limit_bytes=32 * 2**20),
        cost_estimate=pl.CostEstimate(
            flops=400 * rows * rank * features, bytes_accessed=4 * received.size, transcendentals=0
        ),
    )(place, seeds, received, moment_one, moment_two, before)


def gather_kernel(groups, device_list, shares_ref, out_ref, landing, send_sem, recv_sem):
    devices = groups * device_list
    me = lax.axis_index("groups") * device_list + lax.axis_index("dp")

    def place(offset):
        target = lax.rem(me + offset, devices)
        return target, (target // device_list, lax.rem(target, device_list))

    barrier = pltpu.get_barrier_semaphore()

    def greet(offset, carry):
        pl.semaphore_signal(barrier, inc=1, device_id=place(offset)[1], device_id_type=pl.DeviceIdType.MESH)
        return carry

    lax.fori_loop(1, devices, greet, 0)
    pl.semaphore_wait(barrier, devices - 1)

    def send(offset, carry):
        target, where = place(offset)
        pltpu.make_async_remote_copy(
            src_ref=shares_ref.at[target],
            dst_ref=landing.at[offset - 1],
            send_sem=send_sem,
            recv_sem=recv_sem,
            device_id=where,
            device_id_type=pl.DeviceIdType.MESH,
        ).start()
        return carry

    lax.fori_loop(1, devices, send, 0)
    pltpu.make_async_copy(landing, landing, recv_sem).wait()
    out_ref[...] = shares_ref[me] + jnp.sum(landing[...], axis=0)
    pltpu.make_async_copy(landing, landing, send_sem).wait()


def sum_shares(shares, groups, device_list):
    devices, rows, columns = shares.shape
    vmem = pl.BlockSpec(memory_space=pltpu.VMEM)
    return pl.pallas_call(
        functools.partial(gather_kernel, groups, device_list),
        in_specs=[vmem],
        out_specs=vmem,
        out_shape=jax.ShapeDtypeStruct((rows, columns), jnp.float32),
        scratch_shapes=[
            pltpu.VMEM((devices - 1, rows, columns), jnp.float32),
            pltpu.SemaphoreType.DMA,
            pltpu.SemaphoreType.DMA,
        ],
        compiler_params=pltpu.CompilerParams(
            collective_id=0, has_side_effects=True, vmem_limit_bytes=32 * 2**20
        ),
        cost_estimate=pl.CostEstimate(flops=shares.size, bytes_accessed=8 * shares.size, transcendentals=0),
    )(shares)


def local(
    hidden_input_rows,
    rank_cotangent,
    token_identifiers,
    adam_first_moment,
    adam_second_moment,
    block_seeds,
):
    axes = ("groups", "dp")
    groups = lax.axis_size("groups")
    device_list = lax.axis_size("dp")
    my_group = lax.axis_index("groups")
    my_index = lax.axis_index("dp")
    hidden_width = hidden_input_rows.shape[1]
    rank = rank_cotangent.shape[1]
    local_rows = adam_first_moment.shape[0]
    owned = local_rows // groups
    half = owned // 2
    first = max(8, half // 4)
    pieces = ((0, first), (first, half - first))
    devices = groups * device_list
    sequences = devices // 2
    scale = 1.0 / math.sqrt(hidden_width * rank)

    padding_mask = (token_identifiers != 0).astype(jnp.bfloat16)
    masked_values = rank_cotangent * padding_mask[:, None]
    side = jnp.reshape(my_index % 2, (1,)).astype(jnp.int32)
    blocks = half_gradients(hidden_input_rows, masked_values, side, device_list, groups, half, pieces)
    chunks = len(pieces)
    pairs = [(source, source ^ 1) for source in range(device_list)]
    received = []
    for chunk, (_, piece) in enumerate(pieces):
        other = lax.ppermute(blocks[chunks + chunk], "dp", pairs)
        summed = (blocks[chunk] + other).reshape(devices, piece, rank)
        gathered = lax.all_to_all(summed, axes, split_axis=0, concat_axis=0, tiled=True)
        received.append(gathered.reshape(devices * piece, rank))

    partials = jnp.zeros((sequences, block_seeds.shape[0] * FEAT_BLOCK), jnp.float32)
    for chunk, (offset, piece) in enumerate(pieces):
        in_slice = my_group * owned + offset
        place = jnp.stack([in_slice, my_index * local_rows + in_slice]).astype(jnp.int32)
        partials = project(
            place, block_seeds, received[chunk], adam_first_moment, adam_second_moment, partials,
            sequences, piece, half, scale,
        )
    shares = partials.reshape(devices, 8, -1)
    return sum_shares(shares, groups, device_list).reshape(1, -1)


def solution(mesh):
    in_specs = (
        P(("groups", "dp"), None),
        P(("groups", "dp"), None),
        P(("groups", "dp")),
        P("dp", None),
        P("dp", None),
        P(),
    )
    out_specs = P(("groups", "dp"), None)
    return jax.shard_map(local, mesh=mesh, in_specs=in_specs, out_specs=out_specs, check_vma=False)
```

```python
import functools
import math

import jax
import jax.numpy as jnp
from jax import lax
from jax.experimental import pallas as pl
from jax.experimental.pallas import tpu as pltpu
from jax.sharding import PartitionSpec as P

FEAT_BLOCK = 512


beta_one = 0.9
beta_two = 0.999
epsilon = 1e-08
mix_feature = 1640531527
mix_param = 2028178513
mix_round = 73244475

GRAD_COLUMNS = 1024
TILE_ROWS = 2
BODY_ROWS = 32
AHEAD_BODY = 24
STRIP = 32
PASS_COLUMNS = 256


def wrapped(number):
    number %= 2**32
    return number - 2**32 if number >= 2**31 else number


def grad_kernel(shape, side_ref, hidden_ref, masked_ref, *out_refs):
    local_rows, groups, half, pieces = shape
    chunks = len(pieces)
    product = lax.dot_general(
        hidden_ref[...],
        masked_ref[...],
        (((0,), (0,)), ((), ())),
        preferred_element_type=jnp.float32,
    )
    first = side_ref[0] == 0
    for owner in range(product.shape[0] // local_rows):
        for group in range(groups):
            start = owner * local_rows + group * 2 * half
            for chunk, (offset, piece) in enumerate(pieces):
                low = start + offset
                low_rows = product[low : low + piece]
                high_rows = product[low + half : low + half + piece]
                out_refs[chunk][group, owner] = jnp.where(first, low_rows, high_rows)
                out_refs[chunks + chunk][group, owner] = jnp.where(first, high_rows, low_rows)


def half_gradients(hidden, masked, side, device_list, groups, half, pieces):
    tokens, width = hidden.shape
    rank = masked.shape[1]
    local_rows = width // device_list
    sizes = [piece for _, piece in pieces] * 2
    owners = GRAD_COLUMNS // local_rows
    return pl.pallas_call(
        functools.partial(grad_kernel, (local_rows, groups, half, pieces)),
        grid=(width // GRAD_COLUMNS,),
        in_specs=[
            pl.BlockSpec(memory_space=pltpu.SMEM),
            pl.BlockSpec((tokens, GRAD_COLUMNS), lambda step: (0, step)),
            pl.BlockSpec((tokens, rank), lambda step: (0, 0)),
        ],
        out_specs=[
            pl.BlockSpec((groups, owners, size, rank), lambda step: (0, step, 0, 0)) for size in sizes
        ],
        out_shape=[
            jax.ShapeDtypeStruct((groups, device_list, size, rank), jnp.float32) for size in sizes
        ],
        compiler_params=pltpu.CompilerParams(vmem_limit_bytes=32 * 2**20),
        cost_estimate=pl.CostEstimate(
            flops=2 * tokens * width * rank, bytes_accessed=2 * tokens * width + 4 * width * rank, transcendentals=0
        ),
    )(side, hidden, masked)


def sign_strip(hashed):
    hashed = hashed ^ lax.shift_right_logical(hashed, jnp.full_like(hashed, 16))
    hashed = hashed * mix_round
    hashed = hashed ^ lax.shift_right_logical(hashed, jnp.full_like(hashed, 16))
    hashed = hashed * mix_round
    return jnp.where(hashed < 0, -1.0, 1.0).astype(jnp.bfloat16)


def fill_base(block_number, seeds_ref, base):
    column = lax.broadcasted_iota(jnp.int32, base.shape, 0)
    feature = block_number * FEAT_BLOCK + lax.broadcasted_iota(jnp.int32, base.shape, 1)
    base[...] = seeds_ref[block_number] + feature * mix_feature + column * mix_param


def row_offset(row, piece, half, rank, place_ref):
    side = row // piece
    return (place_ref[1] + side * half + (row - side * piece)) * jnp.int32(wrapped(mix_param * rank))


def sign_tile(base, row, columns, piece, half, place_ref):
    rank = base.shape[0]
    return jnp.concatenate(
        [
            sign_strip(
                base[strip : strip + STRIP, columns] + row_offset(row + step, piece, half, rank, place_ref)
            )
            for step in range(TILE_ROWS)
            for strip in range(0, rank, STRIP)
        ],
        axis=0,
    )


def column_parts():
    return [slice(start, start + PASS_COLUMNS) for start in range(0, FEAT_BLOCK, PASS_COLUMNS)]


def ahead_kernel(shape, place_ref, seeds_ref, out_ref, base):
    piece, half, body_rows = shape
    fill_base(pl.program_id(0), seeds_ref, base)
    depth = TILE_ROWS * base.shape[0]
    for index in range(2 * piece // body_rows):
        row = (index + 1) * body_rows - TILE_ROWS
        for columns in column_parts():
            out_ref[index * depth : (index + 1) * depth, columns] = sign_tile(
                base, row, columns, piece, half, place_ref
            )


def hash_ahead(place, seeds, piece, half, rank, body_rows):
    features = seeds.shape[0] * FEAT_BLOCK
    depth = 2 * piece // body_rows * TILE_ROWS * rank
    return pl.pallas_call(
        functools.partial(ahead_kernel, (piece, half, body_rows)),
        grid=(seeds.shape[0],),
        in_specs=[pl.BlockSpec(memory_space=pltpu.SMEM)] * 2,
        out_specs=pl.BlockSpec((depth, FEAT_BLOCK), lambda block: (0, block)),
        out_shape=jax.ShapeDtypeStruct((depth, features), jnp.bfloat16),
        scratch_shapes=[pltpu.VMEM((rank, FEAT_BLOCK), jnp.int32)],
        compiler_params=pltpu.CompilerParams(vmem_limit_bytes=32 * 2**20),
        cost_estimate=pl.CostEstimate(
            flops=1600 * depth * features, bytes_accessed=2 * depth * features, transcendentals=0
        ),
    )(place, seeds)


def project_kernel(
    shape, place_ref, seeds_ref, grad_ref, one_ref, two_ref, before_ref, *refs,
):
    ahead_ref = refs[0] if len(refs) == 4 else None
    out_ref, directions, base = refs[-3:]
    sequences, piece, half, rank, scale, body_rows = shape
    block_number = pl.program_id(0)
    rows = 2 * piece

    @pl.when(block_number == 0)
    def _():
        for side in range(2):
            def prepare(row, carry, side=side):
                gradient = grad_ref[pl.ds(side * piece + row, sequences, stride=rows), :]
                at = pl.ds(place_ref[0] + side * half + row, 1)
                moment_one = beta_one * one_ref[at, :] + (1 - beta_one) * gradient
                moment_two = beta_two * two_ref[at, :] + (1 - beta_two) * gradient * gradient
                direction = moment_one / (jnp.sqrt(moment_two) + epsilon)
                directions[side * piece + row] = direction.astype(jnp.bfloat16)
                return carry

            lax.fori_loop(0, piece, prepare, 0)

    fill_base(block_number, seeds_ref, base)
    depth = TILE_ROWS * rank
    parts = column_parts()

    def body(index, sums):
        sums = list(sums)
        for tile in range(body_rows // TILE_ROWS):
            row = index * body_rows + tile * TILE_ROWS
            directed = jnp.concatenate(
                [directions[row + step] for step in range(TILE_ROWS)], axis=1
            )
            ready = ahead_ref is not None and tile == body_rows // TILE_ROWS - 1
            for part, columns in enumerate(parts):
                if ready:
                    signs = ahead_ref[pl.ds(pl.multiple_of(index * depth, depth), depth), columns]
                else:
                    signs = sign_tile(base, row, columns, piece, half, place_ref)
                sums[part] += jnp.dot(directed, signs, preferred_element_type=jnp.float32)
        return tuple(sums)

    zero = jnp.zeros((sequences, PASS_COLUMNS), jnp.float32)
    sums = lax.fori_loop(0, rows // body_rows, body, (zero,) * len(parts))
    out_ref[...] = before_ref[...] + jnp.concatenate(sums, axis=1) * scale


def project(
    place, seeds, received, moment_one, moment_two, before, ahead, sequences, piece, half, scale, body_rows
):
    rank = received.shape[1]
    features = seeds.shape[0] * FEAT_BLOCK
    rows = 2 * piece
    whole = lambda array: pl.BlockSpec(array.shape, lambda block: (0, 0))
    part = pl.BlockSpec((sequences, FEAT_BLOCK), lambda block: (0, block))
    return pl.pallas_call(
        functools.partial(project_kernel, (sequences, piece, half, rank, scale, body_rows)),
        grid=(seeds.shape[0],),
        in_specs=[
            pl.BlockSpec(memory_space=pltpu.SMEM),
            pl.BlockSpec(memory_space=pltpu.SMEM),
            whole(received),
            whole(moment_one),
            whole(moment_two),
            part,
        ]
        + [pl.BlockSpec((array.shape[0], FEAT_BLOCK), lambda block: (0, block)) for array in ahead],
        out_specs=part,
        out_shape=jax.ShapeDtypeStruct((sequences, features), jnp.float32),
        scratch_shapes=[
            pltpu.VMEM((rows, sequences, rank), jnp.bfloat16),
            pltpu.VMEM((rank, FEAT_BLOCK), jnp.int32),
        ],
        compiler_params=pltpu.CompilerParams(vmem_limit_bytes=32 * 2**20),
        cost_estimate=pl.CostEstimate(
            flops=400 * rows * rank * features, bytes_accessed=4 * received.size, transcendentals=0
        ),
    )(place, seeds, received, moment_one, moment_two, before, *ahead)


def gather_kernel(groups, device_list, shares_ref, out_ref, landing, send_sem, recv_sem):
    devices = groups * device_list
    me = lax.axis_index("groups") * device_list + lax.axis_index("dp")

    def place(offset):
        target = lax.rem(me + offset, devices)
        return target, (target // device_list, lax.rem(target, device_list))

    barrier = pltpu.get_barrier_semaphore()

    def greet(offset, carry):
        pl.semaphore_signal(barrier, inc=1, device_id=place(offset)[1], device_id_type=pl.DeviceIdType.MESH)
        return carry

    lax.fori_loop(1, devices, greet, 0)
    pl.semaphore_wait(barrier, devices - 1)

    def send(offset, carry):
        target, where = place(offset)
        pltpu.make_async_remote_copy(
            src_ref=shares_ref.at[target],
            dst_ref=landing.at[offset - 1],
            send_sem=send_sem,
            recv_sem=recv_sem,
            device_id=where,
            device_id_type=pl.DeviceIdType.MESH,
        ).start()
        return carry

    lax.fori_loop(1, devices, send, 0)
    pltpu.make_async_copy(landing, landing, recv_sem).wait()
    out_ref[...] = shares_ref[me] + jnp.sum(landing[...], axis=0)
    pltpu.make_async_copy(landing, landing, send_sem).wait()


def sum_shares(shares, groups, device_list):
    devices, rows, columns = shares.shape
    vmem = pl.BlockSpec(memory_space=pltpu.VMEM)
    return pl.pallas_call(
        functools.partial(gather_kernel, groups, device_list),
        in_specs=[vmem],
        out_specs=vmem,
        out_shape=jax.ShapeDtypeStruct((rows, columns), jnp.float32),
        scratch_shapes=[
            pltpu.VMEM((devices - 1, rows, columns), jnp.float32),
            pltpu.SemaphoreType.DMA,
            pltpu.SemaphoreType.DMA,
        ],
        compiler_params=pltpu.CompilerParams(
            collective_id=0, has_side_effects=True, vmem_limit_bytes=32 * 2**20
        ),
        cost_estimate=pl.CostEstimate(flops=shares.size, bytes_accessed=8 * shares.size, transcendentals=0),
    )(shares)


def local(
    hidden_input_rows,
    rank_cotangent,
    token_identifiers,
    adam_first_moment,
    adam_second_moment,
    block_seeds,
):
    axes = ("groups", "dp")
    groups = lax.axis_size("groups")
    device_list = lax.axis_size("dp")
    my_group = lax.axis_index("groups")
    my_index = lax.axis_index("dp")
    hidden_width = hidden_input_rows.shape[1]
    rank = rank_cotangent.shape[1]
    local_rows = adam_first_moment.shape[0]
    owned = local_rows // groups
    half = owned // 2
    first = max(8, half // 4)
    pieces = ((0, first), (first, half - first))
    devices = groups * device_list
    sequences = devices // 2
    scale = 1.0 / math.sqrt(hidden_width * rank)

    padding_mask = (token_identifiers != 0).astype(jnp.bfloat16)
    masked_values = rank_cotangent * padding_mask[:, None]
    side = jnp.reshape(my_index % 2, (1,)).astype(jnp.int32)
    blocks = half_gradients(hidden_input_rows, masked_values, side, device_list, groups, half, pieces)
    chunks = len(pieces)
    pairs = [(source, source ^ 1) for source in range(device_list)]
    places = []
    for offset, _ in pieces:
        in_slice = my_group * owned + offset
        places.append(jnp.stack([in_slice, my_index * local_rows + in_slice]).astype(jnp.int32))
    partials = jnp.zeros((sequences, block_seeds.shape[0] * FEAT_BLOCK), jnp.float32)
    late_rows = 2 * pieces[1][1]
    late_body = AHEAD_BODY if late_rows % AHEAD_BODY == 0 else math.gcd(late_rows, BODY_ROWS)
    received = []
    ahead = []
    for chunk, (_, piece) in enumerate(pieces):
        other = lax.ppermute(blocks[chunks + chunk], "dp", pairs)
        summed = (blocks[chunk] + other).reshape(devices, piece, rank)
        if chunk == 0:
            late_place, summed = lax.optimization_barrier((places[1], summed))
            ahead = [hash_ahead(late_place, block_seeds, pieces[1][1], half, rank, late_body)]
            partials, *ahead = lax.optimization_barrier((partials, *ahead))
        gathered = lax.all_to_all(summed, axes, split_axis=0, concat_axis=0, tiled=True)
        received.append(gathered.reshape(devices * piece, rank))

    for chunk, (_, piece) in enumerate(pieces):
        body_rows = late_body if chunk else math.gcd(2 * piece, BODY_ROWS)
        partials = project(
            places[chunk], block_seeds, received[chunk], adam_first_moment, adam_second_moment, partials,
            ahead if chunk else [], sequences, piece, half, scale, body_rows,
        )
    shares = partials.reshape(devices, 8, -1)
    return sum_shares(shares, groups, device_list).reshape(1, -1)


def solution(mesh):
    in_specs = (
        P(("groups", "dp"), None),
        P(("groups", "dp"), None),
        P(("groups", "dp")),
        P("dp", None),
        P("dp", None),
        P(),
    )
    out_specs = P(("groups", "dp"), None)
    return jax.shard_map(local, mesh=mesh, in_specs=in_specs, out_specs=out_specs, check_vma=False)
```

```python
import functools
import math

import jax
import jax.numpy as jnp
from jax import lax
from jax.experimental import pallas as pl
from jax.experimental.pallas import tpu as pltpu
from jax.sharding import PartitionSpec as P

FEAT_BLOCK = 512


beta_one = 0.9
beta_two = 0.999
epsilon = 1e-08
mix_feature = 1640531527
mix_param = 2028178513
mix_round = 73244475

GRAD_COLUMNS = 1024
TILE_ROWS = 2
BODY_ROWS = 32
AHEAD_BODY = 24
STRIP = 32
PASS_COLUMNS = 256


def wrapped(number):
    number %= 2**32
    return number - 2**32 if number >= 2**31 else number


def grad_kernel(shape, side_ref, hidden_ref, masked_ref, *out_refs):
    local_rows, groups, half, pieces = shape
    chunks = len(pieces)
    product = lax.dot_general(
        hidden_ref[...],
        masked_ref[...],
        (((0,), (0,)), ((), ())),
        preferred_element_type=jnp.float32,
    )
    first = side_ref[0] == 0
    for owner in range(product.shape[0] // local_rows):
        for group in range(groups):
            start = owner * local_rows + group * 2 * half
            for chunk, (offset, piece) in enumerate(pieces):
                low = start + offset
                low_rows = product[low : low + piece]
                high_rows = product[low + half : low + half + piece]
                out_refs[chunk][group, owner] = jnp.where(first, low_rows, high_rows)
                out_refs[chunks + chunk][group, owner] = jnp.where(first, high_rows, low_rows)


def half_gradients(hidden, masked, side, device_list, groups, half, pieces):
    tokens, width = hidden.shape
    rank = masked.shape[1]
    local_rows = width // device_list
    sizes = [piece for _, piece in pieces] * 2
    owners = GRAD_COLUMNS // local_rows
    return pl.pallas_call(
        functools.partial(grad_kernel, (local_rows, groups, half, pieces)),
        grid=(width // GRAD_COLUMNS,),
        in_specs=[
            pl.BlockSpec(memory_space=pltpu.SMEM),
            pl.BlockSpec((tokens, GRAD_COLUMNS), lambda step: (0, step)),
            pl.BlockSpec((tokens, rank), lambda step: (0, 0)),
        ],
        out_specs=[
            pl.BlockSpec((groups, owners, size, rank), lambda step: (0, step, 0, 0)) for size in sizes
        ],
        out_shape=[
            jax.ShapeDtypeStruct((groups, device_list, size, rank), jnp.float32) for size in sizes
        ],
        compiler_params=pltpu.CompilerParams(vmem_limit_bytes=32 * 2**20),
        cost_estimate=pl.CostEstimate(
            flops=2 * tokens * width * rank, bytes_accessed=2 * tokens * width + 4 * width * rank, transcendentals=0
        ),
    )(side, hidden, masked)


def sign_strip(hashed):
    hashed = hashed ^ lax.shift_right_logical(hashed, jnp.full_like(hashed, 16))
    hashed = hashed * mix_round
    hashed = hashed ^ lax.shift_right_logical(hashed, jnp.full_like(hashed, 16))
    hashed = hashed * mix_round
    return jnp.where(hashed < 0, jnp.bfloat16(-1), jnp.bfloat16(1))


def fill_base(block_number, seeds_ref, base):
    column = lax.broadcasted_iota(jnp.int32, base.shape, 0)
    feature = block_number * FEAT_BLOCK + lax.broadcasted_iota(jnp.int32, base.shape, 1)
    base[...] = seeds_ref[block_number] + feature * mix_feature + column * mix_param


def row_offset(row, piece, half, rank, place_ref):
    side = row // piece
    return (place_ref[1] + side * half + (row - side * piece)) * jnp.int32(wrapped(mix_param * rank))


def sign_tile(base, row, columns, piece, half, place_ref):
    rank = base.shape[0]
    return jnp.concatenate(
        [
            sign_strip(
                base[strip : strip + STRIP, columns] + row_offset(row + step, piece, half, rank, place_ref)
            )
            for step in range(TILE_ROWS)
            for strip in range(0, rank, STRIP)
        ],
        axis=0,
    )


def column_parts():
    return [slice(start, start + PASS_COLUMNS) for start in range(0, FEAT_BLOCK, PASS_COLUMNS)]


def ahead_kernel(shape, place_ref, seeds_ref, out_ref, base):
    piece, half, body_rows = shape
    fill_base(pl.program_id(0), seeds_ref, base)
    depth = TILE_ROWS * base.shape[0]
    for index in range(2 * piece // body_rows):
        row = (index + 1) * body_rows - TILE_ROWS
        for columns in column_parts():
            out_ref[index * depth : (index + 1) * depth, columns] = sign_tile(
                base, row, columns, piece, half, place_ref
            )


def hash_ahead(place, seeds, piece, half, rank, body_rows):
    features = seeds.shape[0] * FEAT_BLOCK
    depth = 2 * piece // body_rows * TILE_ROWS * rank
    return pl.pallas_call(
        functools.partial(ahead_kernel, (piece, half, body_rows)),
        grid=(seeds.shape[0],),
        in_specs=[pl.BlockSpec(memory_space=pltpu.SMEM)] * 2,
        out_specs=pl.BlockSpec((depth, FEAT_BLOCK), lambda block: (0, block)),
        out_shape=jax.ShapeDtypeStruct((depth, features), jnp.bfloat16),
        scratch_shapes=[pltpu.VMEM((rank, FEAT_BLOCK), jnp.int32)],
        compiler_params=pltpu.CompilerParams(vmem_limit_bytes=56 * 2**20),
        cost_estimate=pl.CostEstimate(
            flops=1600 * depth * features, bytes_accessed=2 * depth * features, transcendentals=0
        ),
    )(place, seeds)


def project_kernel(
    shape, place_ref, seeds_ref, grad_ref, one_ref, two_ref, before_ref, *refs,
):
    ahead_ref = refs[0] if len(refs) == 4 else None
    out_ref, directions, base = refs[-3:]
    sequences, piece, half, rank, scale, body_rows = shape
    block_number = pl.program_id(0)
    rows = 2 * piece

    @pl.when(block_number == 0)
    def _():
        for side in range(2):
            def prepare(row, carry, side=side):
                gradient = grad_ref[pl.ds(side * piece + row, sequences, stride=rows), :]
                at = pl.ds(place_ref[0] + side * half + row, 1)
                moment_one = beta_one * one_ref[at, :] + (1 - beta_one) * gradient
                moment_two = beta_two * two_ref[at, :] + (1 - beta_two) * gradient * gradient
                direction = moment_one / (jnp.sqrt(moment_two) + epsilon)
                directions[side * piece + row] = direction.astype(jnp.bfloat16)
                return carry

            lax.fori_loop(0, piece, prepare, 0)

    fill_base(block_number, seeds_ref, base)
    depth = TILE_ROWS * rank
    parts = column_parts()

    def body(index, sums):
        sums = list(sums)
        for tile in range(body_rows // TILE_ROWS):
            row = index * body_rows + tile * TILE_ROWS
            directed = jnp.concatenate(
                [directions[row + step] for step in range(TILE_ROWS)], axis=1
            )
            ready = ahead_ref is not None and tile == body_rows // TILE_ROWS - 1
            for part, columns in enumerate(parts):
                if ready:
                    signs = ahead_ref[pl.ds(pl.multiple_of(index * depth, depth), depth), columns]
                else:
                    signs = sign_tile(base, row, columns, piece, half, place_ref)
                sums[part] += jnp.dot(directed, signs, preferred_element_type=jnp.float32)
        return tuple(sums)

    zero = jnp.zeros((sequences, PASS_COLUMNS), jnp.float32)
    sums = lax.fori_loop(0, rows // body_rows, body, (zero,) * len(parts))
    out_ref[...] = before_ref[...] + jnp.concatenate(sums, axis=1) * scale


def project(
    place, seeds, received, moment_one, moment_two, before, ahead, sequences, piece, half, scale, body_rows
):
    rank = received.shape[1]
    features = seeds.shape[0] * FEAT_BLOCK
    rows = 2 * piece
    whole = lambda array: pl.BlockSpec(array.shape, lambda block: (0, 0))
    part = pl.BlockSpec((sequences, FEAT_BLOCK), lambda block: (0, block))
    return pl.pallas_call(
        functools.partial(project_kernel, (sequences, piece, half, rank, scale, body_rows)),
        grid=(seeds.shape[0],),
        in_specs=[
            pl.BlockSpec(memory_space=pltpu.SMEM),
            pl.BlockSpec(memory_space=pltpu.SMEM),
            whole(received),
            whole(moment_one),
            whole(moment_two),
            part,
        ]
        + [pl.BlockSpec((array.shape[0], FEAT_BLOCK), lambda block: (0, block)) for array in ahead],
        out_specs=part,
        out_shape=jax.ShapeDtypeStruct((sequences, features), jnp.float32),
        scratch_shapes=[
            pltpu.VMEM((rows, sequences, rank), jnp.bfloat16),
            pltpu.VMEM((rank, FEAT_BLOCK), jnp.int32),
        ],
        compiler_params=pltpu.CompilerParams(vmem_limit_bytes=56 * 2**20),
        cost_estimate=pl.CostEstimate(
            flops=400 * rows * rank * features, bytes_accessed=4 * received.size, transcendentals=0
        ),
    )(place, seeds, received, moment_one, moment_two, before, *ahead)


def gather_kernel(groups, device_list, shares_ref, out_ref, landing, send_sem, recv_sem):
    devices = groups * device_list
    me = lax.axis_index("groups") * device_list + lax.axis_index("dp")

    def place(offset):
        target = lax.rem(me + offset, devices)
        return target, (target // device_list, lax.rem(target, device_list))

    barrier = pltpu.get_barrier_semaphore()

    def greet(offset, carry):
        pl.semaphore_signal(barrier, inc=1, device_id=place(offset)[1], device_id_type=pl.DeviceIdType.MESH)
        return carry

    lax.fori_loop(1, devices, greet, 0)
    pl.semaphore_wait(barrier, devices - 1)

    def send(offset, carry):
        target, where = place(offset)
        pltpu.make_async_remote_copy(
            src_ref=shares_ref.at[target],
            dst_ref=landing.at[offset - 1],
            send_sem=send_sem,
            recv_sem=recv_sem,
            device_id=where,
            device_id_type=pl.DeviceIdType.MESH,
        ).start()
        return carry

    lax.fori_loop(1, devices, send, 0)
    pltpu.make_async_copy(landing, landing, recv_sem).wait()
    out_ref[...] = shares_ref[me] + jnp.sum(landing[...], axis=0)
    pltpu.make_async_copy(landing, landing, send_sem).wait()


def sum_shares(shares, groups, device_list):
    devices, rows, columns = shares.shape
    vmem = pl.BlockSpec(memory_space=pltpu.VMEM)
    return pl.pallas_call(
        functools.partial(gather_kernel, groups, device_list),
        in_specs=[vmem],
        out_specs=vmem,
        out_shape=jax.ShapeDtypeStruct((rows, columns), jnp.float32),
        scratch_shapes=[
            pltpu.VMEM((devices - 1, rows, columns), jnp.float32),
            pltpu.SemaphoreType.DMA,
            pltpu.SemaphoreType.DMA,
        ],
        compiler_params=pltpu.CompilerParams(
            collective_id=0, has_side_effects=True, vmem_limit_bytes=32 * 2**20
        ),
        cost_estimate=pl.CostEstimate(flops=shares.size, bytes_accessed=8 * shares.size, transcendentals=0),
    )(shares)


def local(
    hidden_input_rows,
    rank_cotangent,
    token_identifiers,
    adam_first_moment,
    adam_second_moment,
    block_seeds,
):
    axes = ("groups", "dp")
    groups = lax.axis_size("groups")
    device_list = lax.axis_size("dp")
    my_group = lax.axis_index("groups")
    my_index = lax.axis_index("dp")
    hidden_width = hidden_input_rows.shape[1]
    rank = rank_cotangent.shape[1]
    local_rows = adam_first_moment.shape[0]
    owned = local_rows // groups
    half = owned // 2
    first = max(8, half // 4)
    pieces = ((0, first), (first, half - first))
    devices = groups * device_list
    sequences = devices // 2
    scale = 1.0 / math.sqrt(hidden_width * rank)

    padding_mask = (token_identifiers != 0).astype(jnp.bfloat16)
    masked_values = rank_cotangent * padding_mask[:, None]
    side = jnp.reshape(my_index % 2, (1,)).astype(jnp.int32)
    blocks = half_gradients(hidden_input_rows, masked_values, side, device_list, groups, half, pieces)
    chunks = len(pieces)
    pairs = [(source, source ^ 1) for source in range(device_list)]
    places = []
    for offset, _ in pieces:
        in_slice = my_group * owned + offset
        places.append(jnp.stack([in_slice, my_index * local_rows + in_slice]).astype(jnp.int32))
    partials = jnp.zeros((sequences, block_seeds.shape[0] * FEAT_BLOCK), jnp.float32)
    late_rows = 2 * pieces[1][1]
    late_body = AHEAD_BODY if late_rows % AHEAD_BODY == 0 else math.gcd(late_rows, BODY_ROWS)
    received = []
    ahead = []
    for chunk, (_, piece) in enumerate(pieces):
        other = lax.ppermute(blocks[chunks + chunk], "dp", pairs)
        summed = (blocks[chunk] + other).reshape(devices, piece, rank)
        if chunk == 0:
            late_place, summed = lax.optimization_barrier((places[1], summed))
            ahead = [hash_ahead(late_place, block_seeds, pieces[1][1], half, rank, late_body)]
        else:
            summed, *ahead = lax.optimization_barrier((summed, *ahead))
        gathered = lax.all_to_all(summed, axes, split_axis=0, concat_axis=0, tiled=True)
        received.append(gathered.reshape(devices * piece, rank))

    for chunk, (_, piece) in enumerate(pieces):
        body_rows = late_body if chunk else math.gcd(2 * piece, BODY_ROWS)
        partials = project(
            places[chunk], block_seeds, received[chunk], adam_first_moment, adam_second_moment, partials,
            ahead if chunk else [], sequences, piece, half, scale, body_rows,
        )
    shares = partials.reshape(devices, 8, -1)
    return sum_shares(shares, groups, device_list).reshape(1, -1)


def solution(mesh):
    in_specs = (
        P(("groups", "dp"), None),
        P(("groups", "dp"), None),
        P(("groups", "dp")),
        P("dp", None),
        P("dp", None),
        P(),
    )
    out_specs = P(("groups", "dp"), None)
    return jax.shard_map(local, mesh=mesh, in_specs=in_specs, out_specs=out_specs, check_vma=False)
```

```python
import functools
import math

import jax
import jax.numpy as jnp
from jax import lax
from jax.experimental import pallas as pl
from jax.experimental.pallas import tpu as pltpu
from jax.sharding import PartitionSpec as P

FEAT_BLOCK = 512


beta_one = 0.9
beta_two = 0.999
epsilon = 1e-08
mix_feature = 1640531527
mix_param = 2028178513
mix_round = 73244475

GRAD_COLUMNS = 1024
TILE_ROWS = 2
BODY_ROWS = 64
AHEAD_STRIDE = 24
STRIP = 32
PASS_COLUMNS = 256


def wrapped(number):
    number %= 2**32
    return number - 2**32 if number >= 2**31 else number


def grad_kernel(shape, side_ref, hidden_ref, masked_ref, *out_refs):
    local_rows, groups, half, pieces = shape
    chunks = len(pieces)
    product = lax.dot_general(
        hidden_ref[...],
        masked_ref[...],
        (((0,), (0,)), ((), ())),
        preferred_element_type=jnp.float32,
    )
    first = side_ref[0] == 0
    for owner in range(product.shape[0] // local_rows):
        for group in range(groups):
            start = owner * local_rows + group * 2 * half
            for chunk, (offset, piece) in enumerate(pieces):
                low = start + offset
                low_rows = product[low : low + piece]
                high_rows = product[low + half : low + half + piece]
                out_refs[chunk][group, owner] = jnp.where(first, low_rows, high_rows)
                out_refs[chunks + chunk][group, owner] = jnp.where(first, high_rows, low_rows)


def half_gradients(hidden, masked, side, device_list, groups, half, pieces):
    tokens, width = hidden.shape
    rank = masked.shape[1]
    local_rows = width // device_list
    sizes = [piece for _, piece in pieces] * 2
    owners = GRAD_COLUMNS // local_rows
    return pl.pallas_call(
        functools.partial(grad_kernel, (local_rows, groups, half, pieces)),
        grid=(width // GRAD_COLUMNS,),
        in_specs=[
            pl.BlockSpec(memory_space=pltpu.SMEM),
            pl.BlockSpec((tokens, GRAD_COLUMNS), lambda step: (0, step)),
            pl.BlockSpec((tokens, rank), lambda step: (0, 0)),
        ],
        out_specs=[
            pl.BlockSpec((groups, owners, size, rank), lambda step: (0, step, 0, 0)) for size in sizes
        ],
        out_shape=[
            jax.ShapeDtypeStruct((groups, device_list, size, rank), jnp.float32) for size in sizes
        ],
        compiler_params=pltpu.CompilerParams(vmem_limit_bytes=60 * 2**20),
        cost_estimate=pl.CostEstimate(
            flops=2 * tokens * width * rank, bytes_accessed=2 * tokens * width + 4 * width * rank, transcendentals=0
        ),
    )(side, hidden, masked)


def sign_strip(hashed):
    hashed = hashed ^ lax.shift_right_logical(hashed, jnp.full_like(hashed, 16))
    hashed = hashed * mix_round
    hashed = hashed ^ lax.shift_right_logical(hashed, jnp.full_like(hashed, 16))
    hashed = hashed * mix_round
    return jnp.where(hashed < 0, jnp.bfloat16(-1), jnp.bfloat16(1))


def fill_base(block_number, seeds_ref, base):
    column = lax.broadcasted_iota(jnp.int32, base.shape, 0)
    feature = block_number * FEAT_BLOCK + lax.broadcasted_iota(jnp.int32, base.shape, 1)
    base[...] = seeds_ref[block_number] + feature * mix_feature + column * mix_param


def row_offset(row, piece, half, rank, place_ref):
    side = row // piece
    return (place_ref[1] + side * half + (row - side * piece)) * jnp.int32(wrapped(mix_param * rank))


def sign_tile(base, row, columns, piece, half, place_ref):
    rank = base.shape[0]
    return jnp.concatenate(
        [
            sign_strip(
                base[strip : strip + STRIP, columns] + row_offset(row + step, piece, half, rank, place_ref)
            )
            for step in range(TILE_ROWS)
            for strip in range(0, rank, STRIP)
        ],
        axis=0,
    )


def column_parts():
    return [slice(start, start + PASS_COLUMNS) for start in range(0, FEAT_BLOCK, PASS_COLUMNS)]


def ahead_kernel(shape, place_ref, seeds_ref, out_ref, base):
    piece, half, body_rows = shape
    fill_base(pl.program_id(0), seeds_ref, base)
    depth = TILE_ROWS * base.shape[0]
    for index in range(2 * piece // body_rows):
        row = (index + 1) * body_rows - TILE_ROWS
        for columns in column_parts():
            out_ref[index * depth : (index + 1) * depth, columns] = sign_tile(
                base, row, columns, piece, half, place_ref
            )


def hash_ahead(place, seeds, piece, half, rank, body_rows):
    features = seeds.shape[0] * FEAT_BLOCK
    depth = 2 * piece // body_rows * TILE_ROWS * rank
    return pl.pallas_call(
        functools.partial(ahead_kernel, (piece, half, body_rows)),
        grid=(seeds.shape[0],),
        in_specs=[pl.BlockSpec(memory_space=pltpu.SMEM)] * 2,
        out_specs=pl.BlockSpec((depth, FEAT_BLOCK), lambda block: (0, block)),
        out_shape=jax.ShapeDtypeStruct((depth, features), jnp.bfloat16),
        scratch_shapes=[pltpu.VMEM((rank, FEAT_BLOCK), jnp.int32)],
        compiler_params=pltpu.CompilerParams(vmem_limit_bytes=56 * 2**20),
        cost_estimate=pl.CostEstimate(
            flops=1600 * depth * features, bytes_accessed=2 * depth * features, transcendentals=0
        ),
    )(place, seeds)


def project_kernel(
    shape, place_ref, seeds_ref, grad_ref, one_ref, two_ref, before_ref, *refs,
):
    ahead_ref = refs[0] if len(refs) == 4 else None
    out_ref, directions, base = refs[-3:]
    sequences, piece, half, rank, scale, body_rows, stride = shape
    block_number = pl.program_id(0)
    rows = 2 * piece

    @pl.when(block_number == 0)
    def _():
        for side in range(2):
            def prepare(row, carry, side=side):
                gradient = grad_ref[pl.ds(side * piece + row, sequences, stride=rows), :]
                at = pl.ds(place_ref[0] + side * half + row, 1)
                moment_one = beta_one * one_ref[at, :] + (1 - beta_one) * gradient
                moment_two = beta_two * two_ref[at, :] + (1 - beta_two) * gradient * gradient
                direction = moment_one / (jnp.sqrt(moment_two) + epsilon)
                directions[side * piece + row] = direction.astype(jnp.bfloat16)
                return carry

            lax.fori_loop(0, piece, prepare, 0)

    fill_base(block_number, seeds_ref, base)
    depth = TILE_ROWS * rank
    parts = column_parts()

    def body(index, sums):
        sums = list(sums)
        for tile in range(body_rows // TILE_ROWS):
            row = index * body_rows + tile * TILE_ROWS
            directed = jnp.concatenate(
                [directions[row + step] for step in range(TILE_ROWS)], axis=1
            )
            ready = ahead_ref is not None and (tile + 1) * TILE_ROWS % stride == 0
            held = index * (body_rows // stride) + tile * TILE_ROWS // stride
            for part, columns in enumerate(parts):
                if ready:
                    signs = ahead_ref[pl.ds(pl.multiple_of(held * depth, depth), depth), columns]
                else:
                    signs = sign_tile(base, row, columns, piece, half, place_ref)
                sums[part] += jnp.dot(directed, signs, preferred_element_type=jnp.float32)
        return tuple(sums)

    zero = jnp.zeros((sequences, PASS_COLUMNS), jnp.float32)
    sums = lax.fori_loop(0, rows // body_rows, body, (zero,) * len(parts))
    out_ref[...] = before_ref[...] + jnp.concatenate(sums, axis=1) * scale


def project(
    place, seeds, received, moment_one, moment_two, before, ahead, sequences, piece, half, scale, body_rows, stride
):
    rank = received.shape[1]
    features = seeds.shape[0] * FEAT_BLOCK
    rows = 2 * piece
    whole = lambda array: pl.BlockSpec(array.shape, lambda block: (0, 0))
    part = pl.BlockSpec((sequences, FEAT_BLOCK), lambda block: (0, block))
    return pl.pallas_call(
        functools.partial(project_kernel, (sequences, piece, half, rank, scale, body_rows, stride)),
        grid=(seeds.shape[0],),
        in_specs=[
            pl.BlockSpec(memory_space=pltpu.SMEM),
            pl.BlockSpec(memory_space=pltpu.SMEM),
            whole(received),
            whole(moment_one),
            whole(moment_two),
            part,
        ]
        + [pl.BlockSpec((array.shape[0], FEAT_BLOCK), lambda block: (0, block)) for array in ahead],
        out_specs=part,
        out_shape=jax.ShapeDtypeStruct((sequences, features), jnp.float32),
        scratch_shapes=[
            pltpu.VMEM((rows, sequences, rank), jnp.bfloat16),
            pltpu.VMEM((rank, FEAT_BLOCK), jnp.int32),
        ],
        compiler_params=pltpu.CompilerParams(vmem_limit_bytes=56 * 2**20),
        cost_estimate=pl.CostEstimate(
            flops=400 * rows * rank * features, bytes_accessed=4 * received.size, transcendentals=0
        ),
    )(place, seeds, received, moment_one, moment_two, before, *ahead)


def gather_kernel(groups, device_list, shares_ref, out_ref, landing, send_sem, recv_sem):
    devices = groups * device_list
    me = lax.axis_index("groups") * device_list + lax.axis_index("dp")

    def place(offset):
        target = lax.rem(me + offset, devices)
        return target, (target // device_list, lax.rem(target, device_list))

    barrier = pltpu.get_barrier_semaphore()

    def greet(offset, carry):
        pl.semaphore_signal(barrier, inc=1, device_id=place(offset)[1], device_id_type=pl.DeviceIdType.MESH)
        return carry

    lax.fori_loop(1, devices, greet, 0)
    pl.semaphore_wait(barrier, devices - 1)

    def send(offset, carry):
        target, where = place(offset)
        pltpu.make_async_remote_copy(
            src_ref=shares_ref.at[target],
            dst_ref=landing.at[offset - 1],
            send_sem=send_sem,
            recv_sem=recv_sem,
            device_id=where,
            device_id_type=pl.DeviceIdType.MESH,
        ).start()
        return carry

    lax.fori_loop(1, devices, send, 0)
    pltpu.make_async_copy(landing, landing, recv_sem).wait()
    out_ref[...] = shares_ref[me] + jnp.sum(landing[...], axis=0)
    pltpu.make_async_copy(landing, landing, send_sem).wait()


def sum_shares(shares, groups, device_list):
    devices, rows, columns = shares.shape
    vmem = pl.BlockSpec(memory_space=pltpu.VMEM)
    return pl.pallas_call(
        functools.partial(gather_kernel, groups, device_list),
        in_specs=[vmem],
        out_specs=vmem,
        out_shape=jax.ShapeDtypeStruct((rows, columns), jnp.float32),
        scratch_shapes=[
            pltpu.VMEM((devices - 1, rows, columns), jnp.float32),
            pltpu.SemaphoreType.DMA,
            pltpu.SemaphoreType.DMA,
        ],
        compiler_params=pltpu.CompilerParams(
            collective_id=0, has_side_effects=True, vmem_limit_bytes=32 * 2**20
        ),
        cost_estimate=pl.CostEstimate(flops=shares.size, bytes_accessed=8 * shares.size, transcendentals=0),
    )(shares)


def local(
    hidden_input_rows,
    rank_cotangent,
    token_identifiers,
    adam_first_moment,
    adam_second_moment,
    block_seeds,
):
    axes = ("groups", "dp")
    groups = lax.axis_size("groups")
    device_list = lax.axis_size("dp")
    my_group = lax.axis_index("groups")
    my_index = lax.axis_index("dp")
    hidden_width = hidden_input_rows.shape[1]
    rank = rank_cotangent.shape[1]
    local_rows = adam_first_moment.shape[0]
    owned = local_rows // groups
    half = owned // 2
    first = max(8, half // 4)
    pieces = ((0, first), (first, half - first))
    devices = groups * device_list
    sequences = devices // 2
    scale = 1.0 / math.sqrt(hidden_width * rank)

    padding_mask = (token_identifiers != 0).astype(jnp.bfloat16)
    masked_values = rank_cotangent * padding_mask[:, None]
    side = jnp.reshape(my_index % 2, (1,)).astype(jnp.int32)
    blocks = half_gradients(hidden_input_rows, masked_values, side, device_list, groups, half, pieces)
    chunks = len(pieces)
    pairs = [(source, source ^ 1) for source in range(device_list)]
    places = []
    for offset, _ in pieces:
        in_slice = my_group * owned + offset
        places.append(jnp.stack([in_slice, my_index * local_rows + in_slice]).astype(jnp.int32))
    partials = jnp.zeros((sequences, block_seeds.shape[0] * FEAT_BLOCK), jnp.float32)
    late_rows = 2 * pieces[1][1]
    late_stride = AHEAD_STRIDE if late_rows % AHEAD_STRIDE == 0 else math.gcd(late_rows, BODY_ROWS)
    received = []
    ahead = []
    for chunk, (_, piece) in enumerate(pieces):
        other = lax.ppermute(blocks[chunks + chunk], "dp", pairs)
        summed = (blocks[chunk] + other).reshape(devices, piece, rank)
        if chunk == 0:
            late_place, summed = lax.optimization_barrier((places[1], summed))
            ahead = [hash_ahead(late_place, block_seeds, pieces[1][1], half, rank, late_stride)]
        else:
            summed, *ahead = lax.optimization_barrier((summed, *ahead))
        gathered = lax.all_to_all(summed, axes, split_axis=0, concat_axis=0, tiled=True)
        received.append(gathered.reshape(devices * piece, rank))

    for chunk, (_, piece) in enumerate(pieces):
        body_rows = math.gcd(2 * piece, 2 * late_stride if chunk else BODY_ROWS)
        partials = project(
            places[chunk], block_seeds, received[chunk], adam_first_moment, adam_second_moment, partials,
            ahead if chunk else [], sequences, piece, half, scale, body_rows, late_stride,
        )
    shares = partials.reshape(devices, 8, -1)
    return sum_shares(shares, groups, device_list).reshape(1, -1)


def solution(mesh):
    in_specs = (
        P(("groups", "dp"), None),
        P(("groups", "dp"), None),
        P(("groups", "dp")),
        P("dp", None),
        P("dp", None),
        P(),
    )
    out_specs = P(("groups", "dp"), None)
    return jax.shard_map(local, mesh=mesh, in_specs=in_specs, out_specs=out_specs, check_vma=False)
```

```python
import functools
import math

import jax
import jax.numpy as jnp
from jax import lax
from jax.experimental import pallas as pl
from jax.experimental.pallas import tpu as pltpu
from jax.sharding import PartitionSpec as P

FEAT_BLOCK = 512


beta_one = 0.9
beta_two = 0.999
epsilon = 1e-08
mix_feature = 1640531527
mix_param = 2028178513
mix_round = 73244475

GRAD_COLUMNS = 1024
TILE_ROWS = 2
BODY_ROWS = 64
AHEAD_STRIDE = 24
STRIP = 32
PASS_COLUMNS = 256


def wrapped(number):
    number %= 2**32
    return number - 2**32 if number >= 2**31 else number


def grad_kernel(shape, side_ref, hidden_ref, masked_ref, *out_refs):
    local_rows, groups, half, pieces = shape
    chunks = len(pieces)
    product = lax.dot_general(
        hidden_ref[...],
        masked_ref[...],
        (((0,), (0,)), ((), ())),
        preferred_element_type=jnp.float32,
    )
    first = side_ref[0] == 0
    for owner in range(product.shape[0] // local_rows):
        for group in range(groups):
            start = owner * local_rows + group * 2 * half
            for chunk, (offset, piece) in enumerate(pieces):
                low = start + offset
                low_rows = product[low : low + piece]
                high_rows = product[low + half : low + half + piece]
                out_refs[chunk][group, owner] = jnp.where(first, low_rows, high_rows)
                out_refs[chunks + chunk][group, owner] = jnp.where(first, high_rows, low_rows)


def half_gradients(hidden, masked, side, device_list, groups, half, pieces):
    tokens, width = hidden.shape
    rank = masked.shape[1]
    local_rows = width // device_list
    sizes = [piece for _, piece in pieces] * 2
    owners = GRAD_COLUMNS // local_rows
    return pl.pallas_call(
        functools.partial(grad_kernel, (local_rows, groups, half, pieces)),
        grid=(width // GRAD_COLUMNS,),
        in_specs=[
            pl.BlockSpec(memory_space=pltpu.SMEM),
            pl.BlockSpec((tokens, GRAD_COLUMNS), lambda step: (0, step)),
            pl.BlockSpec((tokens, rank), lambda step: (0, 0)),
        ],
        out_specs=[
            pl.BlockSpec((groups, owners, size, rank), lambda step: (0, step, 0, 0)) for size in sizes
        ],
        out_shape=[
            jax.ShapeDtypeStruct((groups, device_list, size, rank), jnp.float32) for size in sizes
        ],
        compiler_params=pltpu.CompilerParams(vmem_limit_bytes=32 * 2**20),
        cost_estimate=pl.CostEstimate(
            flops=2 * tokens * width * rank, bytes_accessed=2 * tokens * width + 4 * width * rank, transcendentals=0
        ),
    )(side, hidden, masked)


def sign_strip(hashed):
    hashed = hashed ^ lax.shift_right_logical(hashed, jnp.full_like(hashed, 16))
    hashed = hashed * mix_round
    hashed = hashed ^ lax.shift_right_logical(hashed, jnp.full_like(hashed, 16))
    hashed = hashed * mix_round
    return jnp.where(hashed < 0, jnp.bfloat16(-1), jnp.bfloat16(1))


def fill_base(block_number, seeds_ref, base):
    column = lax.broadcasted_iota(jnp.int32, base.shape, 0)
    feature = block_number * FEAT_BLOCK + lax.broadcasted_iota(jnp.int32, base.shape, 1)
    base[...] = seeds_ref[block_number] + feature * mix_feature + column * mix_param


def row_offset(row, piece, half, rank, place_ref):
    side = row // piece
    return (place_ref[1] + side * half + (row - side * piece)) * jnp.int32(wrapped(mix_param * rank))


def sign_tile(base, row, columns, piece, half, place_ref):
    rank = base.shape[0]
    return jnp.concatenate(
        [
            sign_strip(
                base[strip : strip + STRIP, columns] + row_offset(row + step, piece, half, rank, place_ref)
            )
            for step in range(TILE_ROWS)
            for strip in range(0, rank, STRIP)
        ],
        axis=0,
    )


def column_parts():
    return [slice(start, start + PASS_COLUMNS) for start in range(0, FEAT_BLOCK, PASS_COLUMNS)]


def ahead_kernel(shape, place_ref, seeds_ref, out_ref, base):
    piece, half, body_rows = shape
    fill_base(pl.program_id(0), seeds_ref, base)
    depth = TILE_ROWS * base.shape[0]
    for index in range(2 * piece // body_rows):
        row = (index + 1) * body_rows - TILE_ROWS
        for columns in column_parts():
            out_ref[index * depth : (index + 1) * depth, columns] = sign_tile(
                base, row, columns, piece, half, place_ref
            )


def hash_ahead(place, seeds, piece, half, rank, body_rows):
    features = seeds.shape[0] * FEAT_BLOCK
    depth = 2 * piece // body_rows * TILE_ROWS * rank
    return pl.pallas_call(
        functools.partial(ahead_kernel, (piece, half, body_rows)),
        grid=(seeds.shape[0],),
        in_specs=[pl.BlockSpec(memory_space=pltpu.SMEM)] * 2,
        out_specs=pl.BlockSpec((depth, FEAT_BLOCK), lambda block: (0, block)),
        out_shape=jax.ShapeDtypeStruct((depth, features), jnp.bfloat16),
        scratch_shapes=[pltpu.VMEM((rank, FEAT_BLOCK), jnp.int32)],
        compiler_params=pltpu.CompilerParams(vmem_limit_bytes=56 * 2**20),
        cost_estimate=pl.CostEstimate(
            flops=1600 * depth * features, bytes_accessed=2 * depth * features, transcendentals=0
        ),
    )(place, seeds)


def project_kernel(
    shape, place_ref, seeds_ref, grad_ref, one_ref, two_ref, before_ref, *refs,
):
    ahead_ref = refs[0] if len(refs) == 4 else None
    out_ref, directions, base = refs[-3:]
    sequences, piece, half, rank, scale, body_rows, stride = shape
    block_number = pl.program_id(0)
    rows = 2 * piece

    @pl.when(block_number == 0)
    def _():
        for side in range(2):
            def prepare(row, carry, side=side):
                gradient = grad_ref[pl.ds(side * piece + row, sequences, stride=rows), :]
                at = pl.ds(place_ref[0] + side * half + row, 1)
                moment_one = beta_one * one_ref[at, :] + (1 - beta_one) * gradient
                moment_two = beta_two * two_ref[at, :] + (1 - beta_two) * gradient * gradient
                direction = moment_one / (jnp.sqrt(moment_two) + epsilon)
                directions[side * piece + row] = direction.astype(jnp.bfloat16)
                return carry

            lax.fori_loop(0, piece, prepare, 0)

    fill_base(block_number, seeds_ref, base)
    depth = TILE_ROWS * rank
    parts = column_parts()

    def body(index, sums):
        sums = list(sums)
        for tile in range(body_rows // TILE_ROWS):
            row = index * body_rows + tile * TILE_ROWS
            directed = jnp.concatenate(
                [directions[row + step] for step in range(TILE_ROWS)], axis=1
            )
            ready = ahead_ref is not None and (tile + 1) * TILE_ROWS % stride == 0
            held = index * (body_rows // stride) + tile * TILE_ROWS // stride
            for part, columns in enumerate(parts):
                if ready:
                    signs = ahead_ref[pl.ds(pl.multiple_of(held * depth, depth), depth), columns]
                else:
                    signs = sign_tile(base, row, columns, piece, half, place_ref)
                sums[part] += jnp.dot(directed, signs, preferred_element_type=jnp.float32)
        return tuple(sums)

    zero = jnp.zeros((sequences, PASS_COLUMNS), jnp.float32)
    sums = lax.fori_loop(0, rows // body_rows, body, (zero,) * len(parts))
    out_ref[...] = before_ref[...] + jnp.concatenate(sums, axis=1) * scale


def project(
    place, seeds, received, moment_one, moment_two, before, ahead, sequences, piece, half, scale, body_rows, stride
):
    rank = received.shape[1]
    features = seeds.shape[0] * FEAT_BLOCK
    rows = 2 * piece
    whole = lambda array: pl.BlockSpec(array.shape, lambda block: (0, 0))
    part = pl.BlockSpec((sequences, FEAT_BLOCK), lambda block: (0, block))
    return pl.pallas_call(
        functools.partial(project_kernel, (sequences, piece, half, rank, scale, body_rows, stride)),
        grid=(seeds.shape[0],),
        in_specs=[
            pl.BlockSpec(memory_space=pltpu.SMEM),
            pl.BlockSpec(memory_space=pltpu.SMEM),
            whole(received),
            whole(moment_one),
            whole(moment_two),
            part,
        ]
        + [pl.BlockSpec((array.shape[0], FEAT_BLOCK), lambda block: (0, block)) for array in ahead],
        out_specs=part,
        out_shape=jax.ShapeDtypeStruct((sequences, features), jnp.float32),
        scratch_shapes=[
            pltpu.VMEM((rows, sequences, rank), jnp.bfloat16),
            pltpu.VMEM((rank, FEAT_BLOCK), jnp.int32),
        ],
        compiler_params=pltpu.CompilerParams(vmem_limit_bytes=56 * 2**20),
        cost_estimate=pl.CostEstimate(
            flops=400 * rows * rank * features, bytes_accessed=4 * received.size, transcendentals=0
        ),
    )(place, seeds, received, moment_one, moment_two, before, *ahead)


def gather_kernel(groups, device_list, shares_ref, out_ref, landing, send_sem, recv_sem):
    devices = groups * device_list
    me = lax.axis_index("groups") * device_list + lax.axis_index("dp")

    def place(offset):
        target = lax.rem(me + offset, devices)
        return target, (target // device_list, lax.rem(target, device_list))

    barrier = pltpu.get_barrier_semaphore()

    def greet(offset, carry):
        pl.semaphore_signal(barrier, inc=1, device_id=place(offset)[1], device_id_type=pl.DeviceIdType.MESH)
        return carry

    lax.fori_loop(1, devices, greet, 0)
    pl.semaphore_wait(barrier, devices - 1)

    def send(offset, carry):
        target, where = place(offset)
        pltpu.make_async_remote_copy(
            src_ref=shares_ref.at[target],
            dst_ref=landing.at[offset - 1],
            send_sem=send_sem,
            recv_sem=recv_sem,
            device_id=where,
            device_id_type=pl.DeviceIdType.MESH,
        ).start()
        return carry

    lax.fori_loop(1, devices, send, 0)
    pltpu.make_async_copy(landing, landing, recv_sem).wait()
    out_ref[...] = shares_ref[me] + jnp.sum(landing[...], axis=0)
    pltpu.make_async_copy(landing, landing, send_sem).wait()


def sum_shares(shares, groups, device_list):
    devices, rows, columns = shares.shape
    vmem = pl.BlockSpec(memory_space=pltpu.VMEM)
    return pl.pallas_call(
        functools.partial(gather_kernel, groups, device_list),
        in_specs=[vmem],
        out_specs=vmem,
        out_shape=jax.ShapeDtypeStruct((rows, columns), jnp.float32),
        scratch_shapes=[
            pltpu.VMEM((devices - 1, rows, columns), jnp.float32),
            pltpu.SemaphoreType.DMA,
            pltpu.SemaphoreType.DMA,
        ],
        compiler_params=pltpu.CompilerParams(
            collective_id=0, has_side_effects=True, vmem_limit_bytes=32 * 2**20
        ),
        cost_estimate=pl.CostEstimate(flops=shares.size, bytes_accessed=8 * shares.size, transcendentals=0),
    )(shares)


def local(
    hidden_input_rows,
    rank_cotangent,
    token_identifiers,
    adam_first_moment,
    adam_second_moment,
    block_seeds,
):
    axes = ("groups", "dp")
    groups = lax.axis_size("groups")
    device_list = lax.axis_size("dp")
    my_group = lax.axis_index("groups")
    my_index = lax.axis_index("dp")
    hidden_width = hidden_input_rows.shape[1]
    rank = rank_cotangent.shape[1]
    local_rows = adam_first_moment.shape[0]
    owned = local_rows // groups
    half = owned // 2
    first = max(8, half // 4)
    pieces = ((0, first), (first, half - first))
    devices = groups * device_list
    sequences = devices // 2
    scale = 1.0 / math.sqrt(hidden_width * rank)

    padding_mask = (token_identifiers != 0).astype(jnp.bfloat16)
    masked_values = rank_cotangent * padding_mask[:, None]
    side = jnp.reshape(my_index % 2, (1,)).astype(jnp.int32)
    blocks = half_gradients(hidden_input_rows, masked_values, side, device_list, groups, half, pieces)
    chunks = len(pieces)
    pairs = [(source, source ^ 1) for source in range(device_list)]
    places = []
    for offset, _ in pieces:
        in_slice = my_group * owned + offset
        places.append(jnp.stack([in_slice, my_index * local_rows + in_slice]).astype(jnp.int32))
    partials = jnp.zeros((sequences, block_seeds.shape[0] * FEAT_BLOCK), jnp.float32)
    late_rows = 2 * pieces[1][1]
    late_stride = AHEAD_STRIDE if late_rows % AHEAD_STRIDE == 0 else math.gcd(late_rows, BODY_ROWS)
    received = []
    ahead = []
    for chunk, (_, piece) in enumerate(pieces):
        other = lax.ppermute(blocks[chunks + chunk], "dp", pairs)
        summed = (blocks[chunk] + other).reshape(devices, piece, rank)
        if chunk == 0:
            late_place, summed = lax.optimization_barrier((places[1], summed))
            ahead = [hash_ahead(late_place, block_seeds, pieces[1][1], half, rank, late_stride)]
        else:
            summed, *ahead = lax.optimization_barrier((summed, *ahead))
        gathered = lax.all_to_all(summed, axes, split_axis=0, concat_axis=0, tiled=True)
        received.append(gathered.reshape(devices * piece, rank))

    for chunk, (_, piece) in enumerate(pieces):
        body_rows = math.gcd(2 * piece, 4 * late_stride if chunk else BODY_ROWS)
        partials = project(
            places[chunk], block_seeds, received[chunk], adam_first_moment, adam_second_moment, partials,
            ahead if chunk else [], sequences, piece, half, scale, body_rows, late_stride,
        )
    shares = partials.reshape(devices, 8, -1)
    return sum_shares(shares, groups, device_list).reshape(1, -1)


def solution(mesh):
    in_specs = (
        P(("groups", "dp"), None),
        P(("groups", "dp"), None),
        P(("groups", "dp")),
        P("dp", None),
        P("dp", None),
        P(),
    )
    out_specs = P(("groups", "dp"), None)
    return jax.shard_map(local, mesh=mesh, in_specs=in_specs, out_specs=out_specs, check_vma=False)
```
